32 devices in a mesh: pipe: 4 (over x, core), bundle: 8 (over z, y).
Axes of the slice: x: 2, y: 2, z: 4, core: 2. Of those that a mesh axis runs over, the one named last changes fastest.
Arguments:
- act_fwd: bfloat16 [4, 512, 8192], P('pipe', 'bundle'), may hold values from -6 to 6
- grad_in: bfloat16 [4, 512, 8192], P('pipe', 'bundle'), may hold values from -6 to 6
- w_gate: bfloat16 [4, 8192, 1024], P('pipe', None, 'bundle'), may hold values from -0.0625 to 0.0625
- w_up: bfloat16 [4, 8192, 1024], P('pipe', None, 'bundle'), may hold values from -0.0625 to 0.0625
- w_down: bfloat16 [4, 1024, 8192], P('pipe', 'bundle'), may hold values from -0.1875 to 0.1875
- saved_gate: bfloat16 [4, 512, 1024], P('pipe', None, 'bundle'), may hold values from -6 to 6
- saved_up: bfloat16 [4, 512, 1024], P('pipe', None, 'bundle'), may hold values from -6 to 6
- mask_fwd: int32 [4, 32, 8], P('pipe'), may hold values from 0 to 1, as said below
- mask_bwd: int32 [4, 32, 8], P('pipe'), may hold values from 0 to 1, as said below
Outputs:
- next_forward: bfloat16 [4, 512, 8192], P('pipe', 'bundle')
- next_backward: bfloat16 [4, 512, 8192], P('pipe', 'bundle')
The draws below stay inside these ranges and needn't reach their ends.
Inputs may be any that keep to these rules, and one draw needn't show every extreme that they name: `mask_fwd`: within the 4 row blocks of one device's tokens (blocks k * 4 to k * 4 + 3), each bundle is active in at most one. `mask_bwd`: within the 4 row blocks of one device's tokens (blocks k * 4 to k * 4 + 3), each bundle is active in at most one.
All inputs are finite; a program needn't handle non-finite values.
Results may differ from the reference program's by a relative error of at most 0.0033.
Values may be sent and summed in bfloat16 or wider, within the bound.
No kernel may reach another device: no remote copies, remote signals or barrier semaphores. Data moves between devices by JAX's collectives and lax.ppermute only.
A program may use at most 128 MiB of HBM per device.

```python
import jax
import jax.numpy as jnp
from jax import lax

D = 8192
BW = 128
BLOCK = 16
BPD = 4
TOKENS = 512
BLOCKS = 32
BUNDLES = 8
UNITS = 1024
N_PIPE = 4
N_BUNDLE = 8


def activity_pattern(key):
    key_pos = jax.random.fold_in(key, 11)
    key_level = jax.random.fold_in(key, 12)
    key_roll = jax.random.fold_in(key, 13)
    key_force = jax.random.fold_in(key, 14)
    position = jax.random.randint(key_pos, (N_PIPE, N_BUNDLE, BUNDLES), 0, BPD)
    level = jax.random.randint(key_level, (N_PIPE, 1, BUNDLES), 1, 5)
    rolled = jax.random.randint(key_roll, (N_PIPE, N_BUNDLE, BUNDLES), 0, 4)
    forced = jax.random.randint(key_force, (N_PIPE, 1, 1), 0, BUNDLES)
    bundle_ids = jnp.arange(BUNDLES, dtype=jnp.int32)[None, None, :]
    device_ids = jnp.arange(N_BUNDLE, dtype=jnp.int32)[None, :, None]
    active = (rolled < level) | (bundle_ids == forced) & (device_ids == 0)
    block_ids = jnp.arange(BPD, dtype=jnp.int32)[None, None, :, None]
    chosen = (position[:, :, None, :] == block_ids) & active[:, :, None, :]
    return chosen.astype(jnp.int32).reshape(N_PIPE, BLOCKS, BUNDLES)


def draw_mask_fwd(key, part):
    return activity_pattern(jax.random.fold_in(key, 1))


def draw_mask_bwd(key, part):
    return activity_pattern(jax.random.fold_in(key, 2))


def level_of(stream_key, shape, pieces, low, top_value):
    factor_of, own = 1.0, jax.random.fold_in(stream_key, 6)
    for dim, parts in pieces:
        steps = jnp.exp(jax.random.uniform(jax.random.fold_in(own, dim), (parts,), jnp.float32, low / len(pieces), top_value / len(pieces)))
        factor_of = factor_of * jnp.repeat(steps, shape[dim] // parts).reshape([-1 if axis == dim else 1 for axis in range(len(shape))])
    return factor_of


def centred(stream_key, dims, scale, bound, pieces=(), held_as=jnp.bfloat16):
    level = level_of(stream_key, dims, pieces, -0.22, 0.18) if pieces else 1.0
    values = jax.random.normal(stream_key, dims, jnp.float32) * scale * level
    return jnp.minimum(jnp.maximum(values, -bound), bound).astype(held_as)


def setup_inputs(seed: int = 0) -> dict:
    key_of = jax.random.split(jax.random.key(seed), 10)
    return {
        "act_fwd": centred(key_of[0], (N_PIPE, TOKENS, D), 1.0, 6.0, ((0, 4), (1, 8))),
        "grad_in": centred(key_of[1], (N_PIPE, TOKENS, D), 1.0, 6.0, ((0, 4), (1, 8))),
        "w_gate": centred(key_of[2], (N_PIPE, D, UNITS), D ** -0.5, 0.0625, ((0, 4), (2, 8))),
        "w_up": centred(key_of[3], (N_PIPE, D, UNITS), D ** -0.5, 0.0625, ((0, 4), (2, 8))),
        "w_down": centred(key_of[4], (N_PIPE, UNITS, D), UNITS ** -0.5, 0.1875, ((0, 4), (1, 8))),
        "saved_gate": centred(key_of[5], (N_PIPE, TOKENS, UNITS), 1.0, 6.0, ((0, 4), (2, 8))),
        "saved_up": centred(key_of[6], (N_PIPE, TOKENS, UNITS), 1.0, 6.0, ((0, 4), (2, 8))),
        "mask_fwd": draw_mask_fwd(jax.random.fold_in(key_of[9], 71), 0),
        "mask_bwd": draw_mask_bwd(jax.random.fold_in(key_of[9], 71), 0),
    }


def unit_mask_of(mask_blocks):
    rows_mask = jnp.repeat(mask_blocks, BLOCK, axis=0)
    return jnp.repeat(rows_mask, BW, axis=1).astype(jnp.float32)


def forward_section(act_rows, gate_weight, up_weight, down_weight, mask_blocks):
    unit_mask = unit_mask_of(mask_blocks)
    gate_pre = jnp.dot(act_rows, gate_weight, preferred_element_type=jnp.float32)
    up_pre = jnp.dot(act_rows, up_weight, preferred_element_type=jnp.float32)
    hidden = (jnp.maximum(gate_pre, 0.0) * up_pre * unit_mask).astype(jnp.bfloat16)
    hidden_split = hidden.reshape(TOKENS, BUNDLES, BW).transpose(1, 0, 2)
    down_split = down_weight.reshape(BUNDLES, BW, D)

    def add_bundle(total, pair):
        piece = jnp.dot(pair[0], pair[1], preferred_element_type=jnp.float32).astype(jnp.bfloat16)
        piece = lax.optimization_barrier(piece)
        return total + piece.astype(jnp.float32), None

    total, unused = lax.scan(add_bundle, jnp.zeros((TOKENS, D), jnp.float32), (hidden_split, down_split))
    return (act_rows.astype(jnp.float32) + total).astype(jnp.bfloat16)


def backward_section(grad_rows, gate_weight, up_weight, down_weight, saved_gate, saved_up, mask_blocks):
    unit_mask = unit_mask_of(mask_blocks)
    grad_hidden = jnp.dot(grad_rows, down_weight.T, preferred_element_type=jnp.float32)
    gate_value = saved_gate.astype(jnp.float32)
    up_value = saved_up.astype(jnp.float32)
    grad_gate = (jnp.where(gate_value > 0, grad_hidden * up_value, 0.0) * unit_mask).astype(jnp.bfloat16)
    grad_up = (grad_hidden * jnp.maximum(gate_value, 0.0) * unit_mask).astype(jnp.bfloat16)
    gate_split = grad_gate.reshape(TOKENS, BUNDLES, BW).transpose(1, 0, 2)
    up_split = grad_up.reshape(TOKENS, BUNDLES, BW).transpose(1, 0, 2)
    wgate_split = gate_weight.reshape(D, BUNDLES, BW).transpose(1, 0, 2)
    wup_split = up_weight.reshape(D, BUNDLES, BW).transpose(1, 0, 2)

    def add_bundle(total, quad):
        piece = jnp.dot(quad[0], quad[2].T, preferred_element_type=jnp.float32)
        piece = piece + jnp.dot(quad[1], quad[3].T, preferred_element_type=jnp.float32)
        piece = lax.optimization_barrier(piece.astype(jnp.bfloat16))
        return total + piece.astype(jnp.float32), None

    total, unused = lax.scan(add_bundle, jnp.zeros((TOKENS, D), jnp.float32), (gate_split, up_split, wgate_split, wup_split))
    return (grad_rows.astype(jnp.float32) + total).astype(jnp.bfloat16)


def reference(act_fwd, grad_in, w_gate, w_up, w_down, saved_gate, saved_up, mask_fwd, mask_bwd):
    def per_section(section_args):
        act_rows, grad_rows, gate_w, up_w, down_w, gate_saved, up_saved, mask_first, mask_second = section_args
        ahead = forward_section(act_rows, gate_w, up_w, down_w, mask_first)
        behind = backward_section(grad_rows, gate_w, up_w, down_w, gate_saved, up_saved, mask_second)
        return ahead, behind

    ahead, behind = lax.map(per_section, (act_fwd, grad_in, w_gate, w_up, w_down, saved_gate, saved_up, mask_fwd, mask_bwd))
    return jnp.roll(ahead, 1, axis=0), jnp.roll(behind, -1, axis=0)
```

```python
import jax
import jax.numpy as jnp
from jax import lax
from jax.sharding import PartitionSpec as P

BLOCK = 16


def contract_last(left, right):
    return lax.dot_general(
        left, right, (((1,), (1,)), ((), ())), preferred_element_type=jnp.float32
    )


def contract_first(left, right):
    return lax.dot_general(
        left, right, (((0,), (0,)), ((), ())), preferred_element_type=jnp.float32
    )


def one_hot_rows(flags, blocks):
    wide = jnp.repeat(jnp.repeat(flags, BLOCK, axis=0), BLOCK, axis=1)
    row = lax.broadcasted_iota(jnp.int32, wide.shape, 0) % BLOCK
    col = lax.broadcasted_iota(jnp.int32, wide.shape, 1) % BLOCK
    return jnp.where(row == col, wide, 0).astype(jnp.bfloat16)


def exchange(piece, offset):
    count = lax.axis_size("bundle")
    return lax.ppermute(piece, "bundle", [(b, b ^ offset) for b in range(count)])


def deliver(piece, offset, steps):
    pipes, count = lax.axis_size("pipe"), lax.axis_size("bundle")
    pairs = [
        (p * count + b, ((p + steps) % pipes) * count + (b ^ offset))
        for p in range(pipes)
        for b in range(count)
    ]
    return lax.ppermute(piece, ("pipe", "bundle"), pairs)


def far_first(count):
    return list(range(count - 1, -1, -1))


def own_flags(mask, device, blocks_dev, offsets):
    own = lax.dynamic_slice_in_dim(mask[0], device * blocks_dev, blocks_dev, 0)
    return own.T[device ^ offsets]


def owner_flags(mask, device, blocks_dev, offsets):
    blocks = mask.shape[1]
    column = lax.dynamic_slice_in_dim(mask[0], device, 1, 1)[:, 0]
    home = lax.broadcasted_iota(jnp.int32, (offsets.shape[0], blocks), 1) // blocks_dev
    return jnp.where(home == (device ^ offsets)[:, None], column[None, :], 0)


def dispatch(rows, flags, blocks_dev, order):
    packed = jnp.dot(one_hot_rows(flags, blocks_dev), rows, preferred_element_type=jnp.float32)
    packed = packed.astype(jnp.bfloat16)
    arrived = []
    for place, offset in enumerate(order):
        piece = packed[place * BLOCK : (place + 1) * BLOCK]
        arrived.append(exchange(piece, offset) if offset else piece)
    return arrived


def give_back(parts, order, steps):
    return [
        deliver(parts[place * BLOCK : (place + 1) * BLOCK], offset, steps)
        for place, offset in enumerate(order)
    ]


def shifted(value, steps):
    count = lax.axis_size("pipe")
    return lax.ppermute(value, "pipe", [(p, (p + steps) % count) for p in range(count)])


def place_parts(parts, flags, base, blocks_dev):
    total = contract_first(one_hot_rows(flags, blocks_dev), jnp.concatenate(parts, axis=0))
    return (base.astype(jnp.float32) + total).astype(jnp.bfloat16)


def per_device(act_fwd, grad_in, w_gate, w_up, w_down, saved_gate, saved_up, mask_fwd, mask_bwd):
    count = lax.axis_size("bundle")
    device = lax.axis_index("bundle")
    blocks_dev = act_fwd.shape[1] // BLOCK
    gate_w, up_w, down_w = w_gate[0], w_up[0], w_down[0]
    order = far_first(count)
    offsets = jnp.array(order, jnp.int32)
    flags_f = own_flags(mask_fwd, device, blocks_dev, offsets)
    flags_b = own_flags(mask_bwd, device, blocks_dev, offsets)
    rows_f = jnp.concatenate(dispatch(act_fwd[0], flags_f, blocks_dev, order), axis=0)
    rows_b = jnp.concatenate(dispatch(grad_in[0], flags_b, blocks_dev, order), axis=0)
    pick = one_hot_rows(owner_flags(mask_bwd, device, blocks_dev, offsets), mask_bwd.shape[1])
    gate_value = jnp.dot(pick, saved_gate[0], preferred_element_type=jnp.float32)
    up_value = jnp.dot(pick, saved_up[0], preferred_element_type=jnp.float32)

    gate_pre = jnp.dot(rows_f, gate_w, preferred_element_type=jnp.float32)
    up_pre = jnp.dot(rows_f, up_w, preferred_element_type=jnp.float32)
    hidden = (jnp.maximum(gate_pre, 0.0) * up_pre).astype(jnp.bfloat16)
    parts_f = jnp.dot(hidden, down_w, preferred_element_type=jnp.float32).astype(jnp.bfloat16)
    back_f = give_back(parts_f, order, 1)

    grad_hidden = contract_last(rows_b, down_w)
    grad_gate = jnp.where(gate_value > 0, grad_hidden * up_value, 0.0).astype(jnp.bfloat16)
    grad_up = (grad_hidden * jnp.maximum(gate_value, 0.0)).astype(jnp.bfloat16)
    parts_b = (contract_last(grad_gate, gate_w) + contract_last(grad_up, up_w)).astype(jnp.bfloat16)
    back_b = give_back(parts_b, order, -1)

    base_f = shifted(act_fwd[0], 1)
    base_b = shifted(grad_in[0], -1)
    next_flags_f = shifted(flags_f.astype(jnp.float32), 1)
    next_flags_b = shifted(flags_b.astype(jnp.float32), -1)
    next_forward = place_parts(back_f, next_flags_f, base_f, blocks_dev)
    next_backward = place_parts(back_b, next_flags_b, base_b, blocks_dev)
    return (next_forward[None], next_backward[None])


def solution(mesh):
    in_specs = (
        P("pipe", "bundle", None),
        P("pipe", "bundle", None),
        P("pipe", None, "bundle"),
        P("pipe", None, "bundle"),
        P("pipe", "bundle", None),
        P("pipe", None, "bundle"),
        P("pipe", None, "bundle"),
        P("pipe", None, None),
        P("pipe", None, None),
    )
    out_specs = (P("pipe", "bundle", None), P("pipe", "bundle", None))
    return jax.shard_map(
        per_device, mesh=mesh, in_specs=in_specs, out_specs=out_specs, check_vma=False
    )
```

```python
import jax
import jax.numpy as jnp
from jax import lax
from jax.sharding import PartitionSpec as P

BLOCK = 16


def contract_last(left, right):
    return lax.dot_general(
        left, right, (((1,), (1,)), ((), ())), preferred_element_type=jnp.float32
    )


def contract_first(left, right):
    return lax.dot_general(
        left, right, (((0,), (0,)), ((), ())), preferred_element_type=jnp.float32
    )


def one_hot_rows(flags):
    wide = jnp.repeat(jnp.repeat(flags, BLOCK, axis=0), BLOCK, axis=1)
    row = lax.broadcasted_iota(jnp.int32, wide.shape, 0) % BLOCK
    col = lax.broadcasted_iota(jnp.int32, wide.shape, 1) % BLOCK
    return jnp.where(row == col, wide, 0).astype(jnp.bfloat16)


def permute(piece, offset, steps=0, keep=lambda b: True):
    pipes, count = lax.axis_size("pipe"), lax.axis_size("bundle")
    pairs = [
        (p * count + b, ((p + steps) % pipes) * count + (b ^ offset))
        for p in range(pipes)
        for b in range(count)
        if keep(b)
    ]
    return lax.ppermute(piece, ("pipe", "bundle"), pairs)


def permute_where(piece, offset, up, down):
    rising, falling = (lambda b: b < b ^ offset), (lambda b: b > b ^ offset)
    return lax.switch(
        up + 2 * down,
        [
            lambda v: v,
            lambda v: permute(v, offset, 0, rising),
            lambda v: permute(v, offset, 0, falling),
            lambda v: permute(v, offset),
        ],
        piece,
    )


def pair_plan(even, odd):
    act_even, act_odd = even.sum(1), odd.sum(1)
    both = act_even * act_odd * (1 - (even * odd).sum(1))
    first = even + (1 - act_even)[:, None] * odd
    return first, odd * both[:, None], both, act_even, act_odd


def source_plan(mask, source, targets, blocks_dev):
    own = lax.dynamic_slice_in_dim(mask, source * blocks_dev, blocks_dev, 0)
    bundle = lax.broadcasted_iota(jnp.int32, (len(targets), 1, mask.shape[1]), 2)

    def columns(chosen):
        return jnp.where(bundle == chosen[:, None, None], own[None], 0).sum(2)

    return pair_plan(columns(targets & -2), columns(targets | 1))


def owner_plan(mask, device, sources, blocks_dev):
    holder = lax.broadcasted_iota(jnp.int32, (len(sources), mask.shape[1], 1), 1)
    home = holder == sources[:, None, None]

    def blocks_of(bundle):
        column = lax.dynamic_slice_in_dim(mask, bundle, 1, 1).reshape(1, -1, blocks_dev)
        return jnp.where(home, column, 0).sum(1)

    return pair_plan(blocks_of(device & -2), blocks_of(device | 1))


def pieces_of(rows, number):
    return [rows[i * BLOCK : (i + 1) * BLOCK] for i in range(number)]


def dispatch(rows, mask, device, order, blocks_dev):
    offsets = jnp.array(order, jnp.int32)
    first, second, both_out, _, _ = source_plan(mask, device, device ^ offsets, blocks_dev)
    _, _, both_in, _, _ = owner_plan(mask, device, device ^ offsets, blocks_dev)
    pick = one_hot_rows(jnp.concatenate([first, second], axis=0))
    packed = jnp.dot(pick, rows, preferred_element_type=jnp.float32).astype(jnp.bfloat16)
    packed = pieces_of(packed, 2 * len(order))
    odd = device & 1
    mine, other = [], []
    for place, offset in enumerate(order):
        slot_0, slot_1 = packed[place], packed[len(order) + place]
        if offset:
            slot_0 = permute(slot_0, offset)
            low = device < (device ^ offset)
            up = jnp.where(low, both_out[place], both_in[place])
            down = jnp.where(low, both_in[place], both_out[place])
            slot_1 = permute_where(slot_1, offset, up, down)
        mine.append(jnp.where((both_in[place] * odd) > 0, slot_1, slot_0))
        other.append(permute(jnp.where((both_in[place] * (1 - odd)) > 0, slot_1, slot_0), 1))
    return jnp.concatenate(mine + other, axis=0)


def give_back(parts, mask, next_mask, device, order, blocks_dev, steps):
    offsets = jnp.array(order, jnp.int32)
    number = len(order)
    _, _, both, act_even, act_odd = owner_plan(mask, device, device ^ offsets, blocks_dev)
    _, _, next_in, _, _ = source_plan(next_mask, device, device ^ offsets, blocks_dev)
    _, _, next_out, _, _ = owner_plan(next_mask, device, device ^ offsets, blocks_dev)
    odd = device & 1
    pieces = pieces_of(parts, 2 * number)
    slots_0, slots_1 = [], []
    for place, offset in enumerate(order):
        mine, other = pieces[place], permute(pieces[number + place], 1)
        even_part = jnp.where(odd > 0, other, mine)
        odd_part = jnp.where(odd > 0, mine, other)
        odd_first = act_odd[place] * (1 - both[place])
        total = jnp.where(act_even[place] > 0, even_part.astype(jnp.float32), 0.0)
        total = total + jnp.where(odd_first > 0, odd_part.astype(jnp.float32), 0.0)
        slots_0.append(permute(total.astype(jnp.bfloat16), offset, steps))
        slot_1 = permute(odd_part, 0, steps)
        if offset:
            low = device < (device ^ offset)
            up = jnp.where(low, next_out[place], next_in[place])
            down = jnp.where(low, next_in[place], next_out[place])
            slot_1 = permute_where(slot_1, offset, up, down)
        slots_1.append(slot_1)
    return jnp.concatenate(slots_0 + slots_1, axis=0)


def place_parts(slots, next_mask, base, device, order, blocks_dev):
    offsets = jnp.array(order, jnp.int32)
    first, second, _, _, _ = source_plan(next_mask, device, device ^ offsets, blocks_dev)
    total = contract_first(one_hot_rows(jnp.concatenate([first, second], axis=0)), slots)
    return (base.astype(jnp.float32) + total).astype(jnp.bfloat16)


def picked_saved(mask, device, order, blocks_dev):
    offsets = jnp.array(order + [offset ^ 1 for offset in order], jnp.int32)
    column = lax.dynamic_slice_in_dim(mask, device, 1, 1)[:, 0]
    home = lax.broadcasted_iota(jnp.int32, (len(offsets), mask.shape[0]), 1) // blocks_dev
    return one_hot_rows(jnp.where(home == (device ^ offsets)[:, None], column[None, :], 0))


def per_device(act_fwd, grad_in, w_gate, w_up, w_down, saved_gate, saved_up, mask_fwd, mask_bwd):
    count = lax.axis_size("bundle")
    device = lax.axis_index("bundle")
    blocks_dev = act_fwd.shape[1] // BLOCK
    gate_w, up_w, down_w = w_gate[0], w_up[0], w_down[0]
    mask_f, mask_b = mask_fwd[0], mask_bwd[0]
    order = list(range(count - 2, -1, -2))
    next_mask_f, next_mask_b = permute(mask_f, 0, 1), permute(mask_b, 0, -1)
    base_f, base_b = permute(act_fwd[0], 0, 1), permute(grad_in[0], 0, -1)

    rows_f = dispatch(act_fwd[0], mask_f, device, order, blocks_dev)
    rows_b = dispatch(grad_in[0], mask_b, device, order, blocks_dev)
    pick = picked_saved(mask_b, device, order, blocks_dev)
    gate_value = jnp.dot(pick, saved_gate[0], preferred_element_type=jnp.float32)
    up_value = jnp.dot(pick, saved_up[0], preferred_element_type=jnp.float32)

    gate_pre = jnp.dot(rows_f, gate_w, preferred_element_type=jnp.float32)
    up_pre = jnp.dot(rows_f, up_w, preferred_element_type=jnp.float32)
    hidden = (jnp.maximum(gate_pre, 0.0) * up_pre).astype(jnp.bfloat16)
    parts_f = jnp.dot(hidden, down_w, preferred_element_type=jnp.float32).astype(jnp.bfloat16)
    slots_f = give_back(parts_f, mask_f, next_mask_f, device, order, blocks_dev, 1)

    grad_hidden = contract_last(rows_b, down_w)
    grad_gate = jnp.where(gate_value > 0, grad_hidden * up_value, 0.0).astype(jnp.bfloat16)
    grad_up = (grad_hidden * jnp.maximum(gate_value, 0.0)).astype(jnp.bfloat16)
    parts_b = (contract_last(grad_gate, gate_w) + contract_last(grad_up, up_w)).astype(jnp.bfloat16)
    slots_b = give_back(parts_b, mask_b, next_mask_b, device, order, blocks_dev, -1)

    next_forward = place_parts(slots_f, next_mask_f, base_f, device, order, blocks_dev)
    next_backward = place_parts(slots_b, next_mask_b, base_b, device, order, blocks_dev)
    return (next_forward[None], next_backward[None])


def solution(mesh):
    in_specs = (
        P("pipe", "bundle", None),
        P("pipe", "bundle", None),
        P("pipe", None, "bundle"),
        P("pipe", None, "bundle"),
        P("pipe", "bundle", None),
        P("pipe", None, "bundle"),
        P("pipe", None, "bundle"),
        P("pipe", None, None),
        P("pipe", None, None),
    )
    out_specs = (P("pipe", "bundle", None), P("pipe", "bundle", None))
    return jax.shard_map(
        per_device, mesh=mesh, in_specs=in_specs, out_specs=out_specs, check_vma=False
    )
```

```python
import functools

import jax
import jax.numpy as jnp
from jax import lax
from jax.experimental import pallas as pl
from jax.experimental.pallas import tpu as pltpu
from jax.sharding import PartitionSpec as P

BLOCK = 16
OUT, HAS, SAVED = range(3)
FIELDS = 3
VMEM_LIMIT = 48 * 1024 * 1024
ACROSS = ((1,), (1,))


def after(value, *others):
    return lax.optimization_barrier((value, others))[0]


def shifted(value, steps):
    count = lax.axis_size("pipe")
    return lax.ppermute(value, "pipe", [(p, (p + steps) % count) for p in range(count)])


def swap(pieces):
    count = lax.axis_size("bundle")
    pieces = pieces.reshape(count, -1, pieces.shape[1])
    pieces = lax.all_to_all(pieces, "bundle", split_axis=0, concat_axis=0, tiled=True)
    return pieces.reshape(-1, pieces.shape[2])


def plan_one(bundles, blocks_dev, dev, mask, plan):
    def scan(source, bundle):
        active = at = jnp.int32(0)
        for j in range(blocks_dev):
            one = mask[bundle, source * blocks_dev + j]
            active, at = active + one, at + j * one
        return active, at

    for b in range(bundles):
        plan[HAS * bundles + b], plan[OUT * bundles + b] = scan(dev, b)
        plan[SAVED * bundles + b] = b * blocks_dev + scan(b, dev)[1]


def plan_kernel(bundles, blocks_dev, dev_ref, mask_f, mask_b, plan_f, plan_b):
    plan_one(bundles, blocks_dev, dev_ref[0], mask_f, plan_f)
    plan_one(bundles, blocks_dev, dev_ref[0], mask_b, plan_b)


def plans_of(mask_f, mask_b, device, blocks_dev):
    bundles = mask_f.shape[1]
    smem = pl.BlockSpec(memory_space=pltpu.SMEM)
    return pl.pallas_call(
        functools.partial(plan_kernel, bundles, blocks_dev),
        out_shape=[jax.ShapeDtypeStruct((FIELDS * bundles,), jnp.int32)] * 2,
        in_specs=[smem] * 3,
        out_specs=[smem] * 2,
    )(device[None], mask_f.T, mask_b.T)


def chunk_of(width, most):
    chunk = min(width, most)
    while width % chunk:
        chunk //= 2
    return chunk


def chunked(kernel, plan, ins, out_rows, most, scratch=()):
    width = ins[0].shape[1]
    chunk = chunk_of(width, most)

    def spec(rows):
        return pl.BlockSpec((rows, chunk), lambda c, *_: (0, c))

    return pl.pallas_call(
        kernel,
        out_shape=jax.ShapeDtypeStruct((out_rows, width), jnp.bfloat16),
        grid_spec=pltpu.PrefetchScalarGridSpec(
            num_scalar_prefetch=1,
            grid=(width // chunk,),
            in_specs=[spec(a.shape[0]) for a in ins],
            out_specs=spec(out_rows),
            scratch_shapes=[pltpu.VMEM((r, chunk), t) for r, t in scratch],
        ),
        compiler_params=pltpu.CompilerParams(vmem_limit_bytes=VMEM_LIMIT),
    )(plan, *ins)


def block_at(index):
    return pl.ds(pl.multiple_of(index * BLOCK, BLOCK), BLOCK)


def pack(rows, plan, bundles):
    def kernel(plan_ref, rows_ref, out):
        for b in range(bundles):
            out[b * BLOCK : (b + 1) * BLOCK] = rows_ref[block_at(plan_ref[OUT * bundles + b]), :]

    return chunked(kernel, plan, [rows], bundles * BLOCK, 4096)


def placed(plan, base, parts, bundles):
    def kernel(plan_ref, base_ref, parts_ref, out, total):
        total[...] = base_ref[...].astype(jnp.float32)
        for b in range(bundles):
            weight = plan_ref[HAS * bundles + b].astype(jnp.float32)
            part = parts_ref[b * BLOCK : (b + 1) * BLOCK].astype(jnp.float32)
            total[block_at(plan_ref[OUT * bundles + b]), :] += part * weight
        out[...] = total[...].astype(jnp.bfloat16)

    rows = base.shape[0]
    return chunked(kernel, plan, [base, parts], rows, 4096, [(rows, jnp.float32)])


def middle(kernel, plan, rows, weights, saved, first_weights):
    height, width = rows.shape
    chunk = chunk_of(width, 4096)
    steps = width // chunk
    units = min(weights[0].shape)
    specs = [pl.BlockSpec((height, chunk), lambda s, c, *_: (0, jnp.where(s == 0, c, steps - 1)))]
    for i, weight in enumerate(weights):
        tall = weight.shape[0] == width

        def at(s, c, *_, early=i in first_weights, tall=tall):
            where = jnp.where(s == 0, c, steps - 1) if early else jnp.where(s == 0, 0, c)
            return (where, 0) if tall else (0, where)

        shape = (chunk, weight.shape[1]) if tall else (weight.shape[0], chunk)
        specs.append(pl.BlockSpec(shape, at))
    specs += [pl.BlockSpec(a.shape, lambda s, c, *_: (0, 0)) for a in saved]
    return pl.pallas_call(
        kernel,
        out_shape=jax.ShapeDtypeStruct((height, width), jnp.bfloat16),
        grid_spec=pltpu.PrefetchScalarGridSpec(
            num_scalar_prefetch=1,
            grid=(2, steps),
            in_specs=specs,
            out_specs=pl.BlockSpec((height, chunk), lambda s, c, *_: (0, jnp.where(s == 0, 0, c))),
            scratch_shapes=[
                pltpu.VMEM((height, 2 * units), jnp.float32),
                pltpu.VMEM((height, 2 * units), jnp.bfloat16),
            ],
        ),
        compiler_params=pltpu.CompilerParams(vmem_limit_bytes=VMEM_LIMIT),
    )(plan, rows, *weights, *saved)


def dot(left, right, dims=((1,), (0,))):
    return lax.dot_general(left, right, (dims, ((), ())), preferred_element_type=jnp.float32)


def forward(plan, rows, gate_w, up_w, down_w):
    units = gate_w.shape[1]

    def kernel(plan_ref, rows_ref, gate_ref, up_ref, down_ref, out, total_ref, hidden_ref):
        first, start = pl.program_id(0) == 0, pl.program_id(1) == 0

        @pl.when(first & start)
        def _():
            total_ref[...] = jnp.zeros_like(total_ref)

        @pl.when(first)
        def _():
            total_ref[:, :units] += dot(rows_ref[...], gate_ref[...])
            total_ref[:, units:] += dot(rows_ref[...], up_ref[...])

        @pl.when(jnp.logical_not(first) & start)
        def _():
            hidden = jnp.maximum(total_ref[:, :units], 0.0) * total_ref[:, units:]
            hidden_ref[:, :units] = hidden.astype(jnp.bfloat16)

        @pl.when(jnp.logical_not(first))
        def _():
            out[...] = dot(hidden_ref[:, :units], down_ref[...]).astype(jnp.bfloat16)

    return middle(kernel, plan, rows, [gate_w, up_w, down_w], [], (0, 1))


def backward(plan, rows, gate_w, up_w, down_w, saved_gate, saved_up, bundles):
    units = gate_w.shape[1]

    def kernel(
        plan_ref, rows_ref, gate_ref, up_ref, down_ref, gate_saved, up_saved, out, total_ref, grad_ref
    ):
        first, start = pl.program_id(0) == 0, pl.program_id(1) == 0

        @pl.when(first & start)
        def _():
            total_ref[...] = jnp.zeros_like(total_ref)

        @pl.when(first)
        def _():
            total_ref[:, :units] += dot(rows_ref[...], down_ref[...], ACROSS)

        @pl.when(jnp.logical_not(first) & start)
        def _():
            for b in range(bundles):
                place, at = pl.ds(b * BLOCK, BLOCK), block_at(plan_ref[SAVED * bundles + b])
                gate = gate_saved[at, :].astype(jnp.float32)
                up = up_saved[at, :].astype(jnp.float32)
                grad = total_ref[place, :units]
                grad_gate = jnp.where(gate > 0, grad * up, 0.0)
                grad_ref[place, :units] = grad_gate.astype(jnp.bfloat16)
                grad_ref[place, units:] = (grad * jnp.maximum(gate, 0.0)).astype(jnp.bfloat16)

        @pl.when(jnp.logical_not(first))
        def _():
            total = dot(grad_ref[:, :units], gate_ref[...], ACROSS)
            total += dot(grad_ref[:, units:], up_ref[...], ACROSS)
            out[...] = total.astype(jnp.bfloat16)

    return middle(kernel, plan, rows, [gate_w, up_w, down_w], [saved_gate, saved_up], (2,))


def per_device(act_fwd, grad_in, w_gate, w_up, w_down, saved_gate, saved_up, mask_fwd, mask_bwd):
    bundles = lax.axis_size("bundle")
    device = lax.axis_index("bundle")
    blocks_dev = act_fwd.shape[1] // BLOCK
    gate_w, up_w, down_w = w_gate[0], w_up[0], w_down[0]

    plan_f, plan_b = plans_of(mask_fwd[0], mask_bwd[0], device, blocks_dev)
    packed_f = pack(act_fwd[0], plan_f, bundles)
    rows_f = swap(packed_f)
    packed_b = pack(after(grad_in[0], packed_f), plan_b, bundles)
    base_f = shifted(after(act_fwd[0], packed_b), 1)
    base_b = shifted(after(grad_in[0], base_f), -1)
    next_mask_f = shifted(after(mask_fwd[0], packed_b), 1)
    next_mask_b = shifted(after(mask_bwd[0], packed_b), -1)
    next_plan_f, next_plan_b = plans_of(next_mask_f, next_mask_b, device, blocks_dev)

    rows_f = after(rows_f, base_b, next_plan_f)
    rows_b = swap(after(packed_b, rows_f))
    parts_f = shifted(forward(plan_f, rows_f, gate_w, up_w, down_w), 1)
    back_f = swap(after(parts_f, rows_b))
    parts_b = backward(
        plan_b, rows_b, gate_w, up_w, down_w, saved_gate[0], saved_up[0], bundles
    )
    parts_b = shifted(parts_b, -1)
    next_forward = placed(next_plan_f, base_f, back_f, bundles)
    back_b = swap(after(parts_b, back_f))
    next_backward = placed(next_plan_b, base_b, back_b, bundles)
    return (next_forward[None], next_backward[None])


def solution(mesh):
    in_specs = (
        P("pipe", "bundle", None),
        P("pipe", "bundle", None),
        P("pipe", None, "bundle"),
        P("pipe", None, "bundle"),
        P("pipe", "bundle", None),
        P("pipe", None, "bundle"),
        P("pipe", None, "bundle"),
        P("pipe", None, None),
        P("pipe", None, None),
    )
    out_specs = (P("pipe", "bundle", None), P("pipe", "bundle", None))
    return jax.shard_map(
        per_device, mesh=mesh, in_specs=in_specs, out_specs=out_specs, check_vma=False
    )
```

```python
import functools

import jax
import jax.numpy as jnp
from jax import lax
from jax.experimental import pallas as pl
from jax.experimental.pallas import tpu as pltpu
from jax.sharding import PartitionSpec as P

BLOCK = 16
OUT, HAS, SAVED = range(3)
FIELDS = 3
VMEM_LIMIT = 48 * 1024 * 1024
VMEM_MOST = 60 * 1024 * 1024
PLACE_CHUNK = 4096
ACROSS = ((1,), (1,))


def after(value, *others):
    return lax.optimization_barrier((value, others))[0]


def shifted(value, steps):
    count = lax.axis_size("pipe")
    return lax.ppermute(value, "pipe", [(p, (p + steps) % count) for p in range(count)])


def swap(pieces):
    count = lax.axis_size("bundle")
    pieces = pieces.reshape(count, -1, pieces.shape[1])
    pieces = lax.all_to_all(pieces, "bundle", split_axis=0, concat_axis=0, tiled=True)
    return pieces.reshape(-1, pieces.shape[2])


def plan_one(bundles, blocks_dev, dev, mask, plan):
    def scan(source, bundle):
        active = at = jnp.int32(0)
        for j in range(blocks_dev):
            one = mask[bundle, source * blocks_dev + j]
            active, at = active + one, at + j * one
        return active, at

    for b in range(bundles):
        plan[HAS * bundles + b], plan[OUT * bundles + b] = scan(dev, b)
        plan[SAVED * bundles + b] = b * blocks_dev + scan(b, dev)[1]


def plan_kernel(bundles, blocks_dev, dev_ref, mask_f, mask_b, plan_f, plan_b):
    plan_one(bundles, blocks_dev, dev_ref[0], mask_f, plan_f)
    plan_one(bundles, blocks_dev, dev_ref[0], mask_b, plan_b)


def plans_of(mask_f, mask_b, device, blocks_dev):
    bundles = mask_f.shape[1]
    smem = pl.BlockSpec(memory_space=pltpu.SMEM)
    return pl.pallas_call(
        functools.partial(plan_kernel, bundles, blocks_dev),
        out_shape=[jax.ShapeDtypeStruct((FIELDS * bundles,), jnp.int32)] * 2,
        in_specs=[smem] * 3,
        out_specs=[smem] * 2,
    )(device[None], mask_f.T, mask_b.T)


def chunk_of(width, most):
    chunk = min(width, most)
    while width % chunk:
        chunk //= 2
    return chunk


def chunked(kernel, plan, ins, out_rows, most, scratch=()):
    width = ins[0].shape[1]
    chunk = chunk_of(width, most)

    def spec(rows):
        return pl.BlockSpec((rows, chunk), lambda c, *_: (0, c))

    return pl.pallas_call(
        kernel,
        out_shape=jax.ShapeDtypeStruct((out_rows, width), jnp.bfloat16),
        grid_spec=pltpu.PrefetchScalarGridSpec(
            num_scalar_prefetch=1,
            grid=(width // chunk,),
            in_specs=[spec(a.shape[0]) for a in ins],
            out_specs=spec(out_rows),
            scratch_shapes=[pltpu.VMEM((r, chunk), t) for r, t in scratch],
        ),
        compiler_params=pltpu.CompilerParams(vmem_limit_bytes=VMEM_LIMIT),
    )(plan, *ins)


def block_at(index):
    return pl.ds(pl.multiple_of(index * BLOCK, BLOCK), BLOCK)


def pack(rows, mask, device, blocks_dev):
    bundles, width = mask.shape[1], rows.shape[1]
    chunk = chunk_of(width, 4096)

    def kernel(dev_ref, mask_ref, rows_ref, out):
        for b in range(bundles):
            at = jnp.int32(0)
            for j in range(1, blocks_dev):
                at += j * mask_ref[b, dev_ref[0] * blocks_dev + j]
            out[b * BLOCK : (b + 1) * BLOCK] = rows_ref[block_at(at), :]

    return pl.pallas_call(
        kernel,
        out_shape=jax.ShapeDtypeStruct((bundles * BLOCK, width), jnp.bfloat16),
        grid=(width // chunk,),
        in_specs=[
            pl.BlockSpec(memory_space=pltpu.SMEM),
            pl.BlockSpec(memory_space=pltpu.SMEM),
            pl.BlockSpec((rows.shape[0], chunk), lambda c: (0, c)),
        ],
        out_specs=pl.BlockSpec((bundles * BLOCK, chunk), lambda c: (0, c)),
        compiler_params=pltpu.CompilerParams(vmem_limit_bytes=VMEM_MOST),
    )(device[None], mask.T, rows)


def placed(plan, base, parts, bundles):
    rows = base.shape[0]

    def kernel(plan_ref, base_ref, parts_ref, out):
        row = lax.broadcasted_iota(jnp.int32, (rows, bundles * BLOCK), 0)
        part = lax.broadcasted_iota(jnp.int32, (rows, bundles * BLOCK), 1)
        goes = jnp.full_like(row, -1)
        for b in range(bundles):
            first = plan_ref[OUT * bundles + b] * BLOCK - b * BLOCK
            held = (part >= b * BLOCK) & (part < (b + 1) * BLOCK) & (plan_ref[HAS * bundles + b] != 0)
            goes = jnp.where(held, part + first, goes)
        pick = jnp.where(goes == row, 1.0, 0.0).astype(jnp.bfloat16)
        total = base_ref[...].astype(jnp.float32) + dot(pick, parts_ref[...])
        out[...] = total.astype(jnp.bfloat16)

    return chunked(kernel, plan, [base, parts], rows, PLACE_CHUNK)


def middle(kernel, plan, rows, weights, saved, first_weights):
    height, width = rows.shape
    chunk = chunk_of(width, 4096)
    steps = width // chunk
    units = min(weights[0].shape)
    specs = [pl.BlockSpec((height, chunk), lambda s, c, *_: (0, jnp.where(s == 0, c, steps - 1)))]
    for i, weight in enumerate(weights):
        tall = weight.shape[0] == width

        def at(s, c, *_, early=i in first_weights, tall=tall):
            where = jnp.where(s == 0, c, steps - 1) if early else jnp.where(s == 0, 0, c)
            return (where, 0) if tall else (0, where)

        shape = (chunk, weight.shape[1]) if tall else (weight.shape[0], chunk)
        specs.append(pl.BlockSpec(shape, at))
    specs += [pl.BlockSpec(a.shape, lambda s, c, *_: (0, 0)) for a in saved]
    return pl.pallas_call(
        kernel,
        out_shape=jax.ShapeDtypeStruct((height, width), jnp.bfloat16),
        grid_spec=pltpu.PrefetchScalarGridSpec(
            num_scalar_prefetch=1,
            grid=(2, steps),
            in_specs=specs,
            out_specs=pl.BlockSpec((height, chunk), lambda s, c, *_: (0, jnp.where(s == 0, 0, c))),
            scratch_shapes=[
                pltpu.VMEM((height, 2 * units), jnp.float32),
                pltpu.VMEM((height, 2 * units), jnp.bfloat16),
            ],
        ),
        compiler_params=pltpu.CompilerParams(vmem_limit_bytes=VMEM_LIMIT),
    )(plan, rows, *weights, *saved)


def dot(left, right, dims=((1,), (0,))):
    return lax.dot_general(left, right, (dims, ((), ())), preferred_element_type=jnp.float32)


def forward(plan, rows, gate_w, up_w, down_w):
    units = gate_w.shape[1]

    def kernel(plan_ref, rows_ref, gate_ref, up_ref, down_ref, out, total_ref, hidden_ref):
        first, start = pl.program_id(0) == 0, pl.program_id(1) == 0

        @pl.when(first & start)
        def _():
            total_ref[...] = jnp.zeros_like(total_ref)

        @pl.when(first)
        def _():
            total_ref[:, :units] += dot(rows_ref[...], gate_ref[...])
            total_ref[:, units:] += dot(rows_ref[...], up_ref[...])

        @pl.when(jnp.logical_not(first) & start)
        def _():
            hidden = jnp.maximum(total_ref[:, :units], 0.0) * total_ref[:, units:]
            hidden_ref[:, :units] = hidden.astype(jnp.bfloat16)

        @pl.when(jnp.logical_not(first))
        def _():
            out[...] = dot(hidden_ref[:, :units], down_ref[...]).astype(jnp.bfloat16)

    return middle(kernel, plan, rows, [gate_w, up_w, down_w], [], (0, 1))


def backward(plan, rows, gate_w, up_w, down_w, saved_gate, saved_up, bundles):
    units = gate_w.shape[1]

    def kernel(
        plan_ref, rows_ref, gate_ref, up_ref, down_ref, gate_saved, up_saved, out, total_ref, grad_ref
    ):
        first, start = pl.program_id(0) == 0, pl.program_id(1) == 0

        @pl.when(first & start)
        def _():
            total_ref[...] = jnp.zeros_like(total_ref)

        @pl.when(first)
        def _():
            total_ref[:, :units] += dot(rows_ref[...], down_ref[...], ACROSS)

        @pl.when(jnp.logical_not(first) & start)
        def _():
            for b in range(bundles):
                place, at = pl.ds(b * BLOCK, BLOCK), block_at(plan_ref[SAVED * bundles + b])
                gate = gate_saved[at, :].astype(jnp.float32)
                up = up_saved[at, :].astype(jnp.float32)
                grad = total_ref[place, :units]
                grad_gate = jnp.where(gate > 0, grad * up, 0.0)
                grad_ref[place, :units] = grad_gate.astype(jnp.bfloat16)
                grad_ref[place, units:] = (grad * jnp.maximum(gate, 0.0)).astype(jnp.bfloat16)

        @pl.when(jnp.logical_not(first))
        def _():
            total = dot(grad_ref[:, :units], gate_ref[...], ACROSS)
            total += dot(grad_ref[:, units:], up_ref[...], ACROSS)
            out[...] = total.astype(jnp.bfloat16)

    return middle(kernel, plan, rows, [gate_w, up_w, down_w], [saved_gate, saved_up], (2,))


def per_device(act_fwd, grad_in, w_gate, w_up, w_down, saved_gate, saved_up, mask_fwd, mask_bwd):
    bundles = lax.axis_size("bundle")
    device = lax.axis_index("bundle")
    blocks_dev = act_fwd.shape[1] // BLOCK
    gate_w, up_w, down_w = w_gate[0], w_up[0], w_down[0]

    packed_f = pack(act_fwd[0], mask_fwd[0], device, blocks_dev)
    rows_f = swap(packed_f)
    packed_b = pack(after(grad_in[0], packed_f), mask_bwd[0], device, blocks_dev)
    plan_f, plan_b = plans_of(mask_fwd[0], after(mask_bwd[0], packed_b), device, blocks_dev)
    base_f = shifted(after(act_fwd[0], packed_b), 1)
    base_b = shifted(after(grad_in[0], base_f), -1)
    next_mask_f = shifted(after(mask_fwd[0], packed_b), 1)
    next_mask_b = shifted(after(mask_bwd[0], packed_b), -1)
    next_plan_f, next_plan_b = plans_of(next_mask_f, next_mask_b, device, blocks_dev)

    rows_f = after(rows_f, base_b, next_plan_f)
    rows_b = swap(after(packed_b, rows_f))
    parts_f = shifted(forward(plan_f, rows_f, gate_w, up_w, down_w), 1)
    back_f = swap(after(parts_f, rows_b))
    parts_b = backward(
        plan_b, rows_b, gate_w, up_w, down_w, saved_gate[0], saved_up[0], bundles
    )
    parts_b = shifted(parts_b, -1)
    next_forward = placed(next_plan_f, base_f, back_f, bundles)
    back_b = swap(after(parts_b, back_f))
    next_backward = placed(next_plan_b, base_b, back_b, bundles)
    return (next_forward[None], next_backward[None])


def solution(mesh):
    in_specs = (
        P("pipe", "bundle", None),
        P("pipe", "bundle", None),
        P("pipe", None, "bundle"),
        P("pipe", None, "bundle"),
        P("pipe", "bundle", None),
        P("pipe", None, "bundle"),
        P("pipe", None, "bundle"),
        P("pipe", None, None),
        P("pipe", None, None),
    )
    out_specs = (P("pipe", "bundle", None), P("pipe", "bundle", None))
    return jax.shard_map(
        per_device, mesh=mesh, in_specs=in_specs, out_specs=out_specs, check_vma=False
    )
```

```python
import jax
import jax.numpy as jnp
from jax import lax
from jax.experimental import pallas as pl
from jax.experimental.pallas import tpu as pltpu
from jax.sharding import PartitionSpec as P

BLOCK = 16
OUT, HAS, SAVED = range(3)
FIELDS = 3
VMEM_LIMIT = 48 * 1024 * 1024
VMEM_MOST = 60 * 1024 * 1024
VMEM_LEAST = 16 * 1024 * 1024
PLACE_CHUNK = 4096
ACROSS = ((1,), (1,))


def after(value, *others):
    return lax.optimization_barrier((value, others))[0]


def shifted(value, steps):
    count = lax.axis_size("pipe")
    return lax.ppermute(value, "pipe", [(p, (p + steps) % count) for p in range(count)])


def permute(piece, offset):
    count = lax.axis_size("bundle")
    return lax.ppermute(piece, "bundle", [(b, b ^ offset) for b in range(count)])


def swap(pieces):
    count = lax.axis_size("bundle")
    pieces = pieces.reshape(count, -1, pieces.shape[1])
    pieces = lax.all_to_all(pieces, "bundle", split_axis=0, concat_axis=0, tiled=True)
    return pieces.reshape(-1, pieces.shape[2])


def plan_one(bundles, blocks_dev, dev, mask, plan):
    def scan(source, bundle):
        active = at = jnp.int32(0)
        for j in range(blocks_dev):
            one = mask[bundle, source * blocks_dev + j]
            active, at = active + one, at + j * one
        return active, at

    for b in range(bundles):
        plan[HAS * bundles + b], plan[OUT * bundles + b] = scan(dev, b)
        plan[SAVED * bundles + b] = b * blocks_dev + scan(b, dev)[1]
    plan[FIELDS * bundles] = dev


def plans_of(masks, device, blocks_dev):
    bundles, number = masks[0].shape[1], len(masks)

    def kernel(dev_ref, *refs):
        for mask, plan in zip(refs[:number], refs[number:]):
            plan_one(bundles, blocks_dev, dev_ref[0], mask, plan)

    smem = pl.BlockSpec(memory_space=pltpu.SMEM)
    return pl.pallas_call(
        kernel,
        out_shape=[jax.ShapeDtypeStruct((FIELDS * bundles + 1,), jnp.int32)] * number,
        in_specs=[smem] * (1 + number),
        out_specs=[smem] * number,
    )(device[None], *[mask.T for mask in masks])


def chunk_of(width, most):
    chunk = min(width, most)
    while width % chunk:
        chunk //= 2
    return chunk


def chunked(kernel, plan, ins, out_rows, most, scratch=()):
    width = ins[0].shape[1]
    chunk = chunk_of(width, most)

    def spec(rows):
        return pl.BlockSpec((rows, chunk), lambda c, *_: (0, c))

    return pl.pallas_call(
        kernel,
        out_shape=jax.ShapeDtypeStruct((out_rows, width), jnp.bfloat16),
        grid_spec=pltpu.PrefetchScalarGridSpec(
            num_scalar_prefetch=1,
            grid=(width // chunk,),
            in_specs=[spec(a.shape[0]) for a in ins],
            out_specs=spec(out_rows),
            scratch_shapes=[pltpu.VMEM((r, chunk), t) for r, t in scratch],
        ),
        compiler_params=pltpu.CompilerParams(vmem_limit_bytes=VMEM_LEAST),
    )(plan, *ins)


def block_at(index):
    return pl.ds(pl.multiple_of(index * BLOCK, BLOCK), BLOCK)


def pack(rows, mask, device, blocks_dev, order=()):
    bundles, width = mask.shape[1], rows.shape[1]
    chunk = chunk_of(width, 4096)
    out_rows = [BLOCK] * bundles if order else [bundles * BLOCK]

    def kernel(dev_ref, mask_ref, rows_ref, *outs):
        for i in range(bundles):
            bundle = dev_ref[0] ^ order[i] if order else i
            at = jnp.int32(0)
            for j in range(1, blocks_dev):
                at += j * mask_ref[bundle, dev_ref[0] * blocks_dev + j]
            out = outs[i] if order else outs[0].at[pl.ds(i * BLOCK, BLOCK)]
            out[...] = rows_ref[block_at(at), :]

    return pl.pallas_call(
        kernel,
        out_shape=[jax.ShapeDtypeStruct((r, width), jnp.bfloat16) for r in out_rows],
        grid=(width // chunk,),
        in_specs=[
            pl.BlockSpec(memory_space=pltpu.SMEM),
            pl.BlockSpec(memory_space=pltpu.SMEM),
            pl.BlockSpec((rows.shape[0], chunk), lambda c: (0, c)),
        ],
        out_specs=[pl.BlockSpec((r, chunk), lambda c: (0, c)) for r in out_rows],
        compiler_params=pltpu.CompilerParams(vmem_limit_bytes=VMEM_MOST),
    )(device[None], mask.T, rows)


def placed(plan, base, parts, bundles):
    rows = base.shape[0]

    def kernel(plan_ref, base_ref, parts_ref, out):
        row = lax.broadcasted_iota(jnp.int32, (rows, bundles * BLOCK), 0)
        part = lax.broadcasted_iota(jnp.int32, (rows, bundles * BLOCK), 1)
        goes = jnp.full_like(row, -1)
        for b in range(bundles):
            first = plan_ref[OUT * bundles + b] * BLOCK - b * BLOCK
            held = (part >= b * BLOCK) & (part < (b + 1) * BLOCK) & (plan_ref[HAS * bundles + b] != 0)
            goes = jnp.where(held, part + first, goes)
        pick = jnp.where(goes == row, 1.0, 0.0).astype(jnp.bfloat16)
        total = base_ref[...].astype(jnp.float32) + dot(pick, parts_ref[...])
        out[...] = total.astype(jnp.bfloat16)

    return chunked(kernel, plan, [base, parts], rows, PLACE_CHUNK)


def copied(value):
    def kernel(value_ref, out):
        out[...] = value_ref[...]

    chunk = chunk_of(value.shape[1], 4096)
    spec = pl.BlockSpec((value.shape[0], chunk), lambda c: (0, c))
    return pl.pallas_call(
        kernel,
        out_shape=jax.ShapeDtypeStruct(value.shape, value.dtype),
        grid=(value.shape[1] // chunk,),
        in_specs=[spec],
        out_specs=spec,
        compiler_params=pltpu.CompilerParams(vmem_limit_bytes=VMEM_MOST),
    )(value)


def middle(kernel, plan, rows, weights, saved, first_weights):
    width = rows[0].shape[1]
    height = sum(piece.shape[0] for piece in rows)
    chunk = chunk_of(width, 4096)
    steps = width // chunk
    units = min(weights[0].shape)
    specs = [
        pl.BlockSpec((piece.shape[0], chunk), lambda s, c, *_: (0, jnp.where(s == 0, c, steps - 1)))
        for piece in rows
    ]
    for i, weight in enumerate(weights):
        tall = weight.shape[0] == width

        def at(s, c, *_, early=i in first_weights, tall=tall):
            where = jnp.where(s == 0, c, steps - 1) if early else jnp.where(s == 0, 0, c)
            return (where, 0) if tall else (0, where)

        shape = (chunk, weight.shape[1]) if tall else (weight.shape[0], chunk)
        specs.append(pl.BlockSpec(shape, at))
    specs += [pl.BlockSpec(a.shape, lambda s, c, *_: (0, 0)) for a in saved]
    return pl.pallas_call(
        kernel,
        out_shape=jax.ShapeDtypeStruct((height, width), jnp.bfloat16),
        grid_spec=pltpu.PrefetchScalarGridSpec(
            num_scalar_prefetch=1,
            grid=(2, steps),
            in_specs=specs,
            out_specs=pl.BlockSpec((height, chunk), lambda s, c, *_: (0, jnp.where(s == 0, 0, c))),
            scratch_shapes=[
                pltpu.VMEM((height, chunk), jnp.bfloat16),
                pltpu.VMEM((height, 2 * units), jnp.float32),
                pltpu.VMEM((height, 2 * units), jnp.bfloat16),
            ],
        ),
        compiler_params=pltpu.CompilerParams(vmem_limit_bytes=VMEM_LIMIT),
    )(plan, *rows, *weights, *saved)


def dot(left, right, dims=((1,), (0,))):
    return lax.dot_general(left, right, (dims, ((), ())), preferred_element_type=jnp.float32)


def forward(plan, rows, gate_w, up_w, down_w):
    units = gate_w.shape[1]

    def kernel(plan_ref, rows_ref, gate_ref, up_ref, down_ref, out, _, total_ref, hidden_ref):
        first, start = pl.program_id(0) == 0, pl.program_id(1) == 0

        @pl.when(first & start)
        def _():
            total_ref[...] = jnp.zeros_like(total_ref)

        @pl.when(first)
        def _():
            total_ref[:, :units] += dot(rows_ref[...], gate_ref[...])
            total_ref[:, units:] += dot(rows_ref[...], up_ref[...])

        @pl.when(jnp.logical_not(first) & start)
        def _():
            hidden = jnp.maximum(total_ref[:, :units], 0.0) * total_ref[:, units:]
            hidden_ref[:, :units] = hidden.astype(jnp.bfloat16)

        @pl.when(jnp.logical_not(first))
        def _():
            out[...] = dot(hidden_ref[:, :units], down_ref[...]).astype(jnp.bfloat16)

    return middle(kernel, plan, [rows], [gate_w, up_w, down_w], [], (0, 1))


def backward(plan, pieces, gate_w, up_w, down_w, saved_gate, saved_up, order):
    bundles = len(order)
    units = gate_w.shape[1]

    def kernel(plan_ref, *refs):
        ins, refs = refs[:bundles], refs[bundles:]
        gate_ref, up_ref, down_ref, gate_saved, up_saved, out, rows_ref, total_ref, grad_ref = refs
        first, start = pl.program_id(0) == 0, pl.program_id(1) == 0

        @pl.when(first & start)
        def _():
            total_ref[...] = jnp.zeros_like(total_ref)

        @pl.when(first)
        def _():
            for i, piece in enumerate(ins):
                at = block_at(plan_ref[FIELDS * bundles] ^ order[i])
                rows_ref[at, :] = piece[...]
            total_ref[:, :units] += dot(rows_ref[...], down_ref[...], ACROSS)

        @pl.when(jnp.logical_not(first) & start)
        def _():
            for b in range(bundles):
                place, at = pl.ds(b * BLOCK, BLOCK), block_at(plan_ref[SAVED * bundles + b])
                gate = gate_saved[at, :].astype(jnp.float32)
                up = up_saved[at, :].astype(jnp.float32)
                grad = total_ref[place, :units]
                grad_gate = jnp.where(gate > 0, grad * up, 0.0)
                grad_ref[place, :units] = grad_gate.astype(jnp.bfloat16)
                grad_ref[place, units:] = (grad * jnp.maximum(gate, 0.0)).astype(jnp.bfloat16)

        @pl.when(jnp.logical_not(first))
        def _():
            total = dot(grad_ref[:, :units], gate_ref[...], ACROSS)
            total += dot(grad_ref[:, units:], up_ref[...], ACROSS)
            out[...] = total.astype(jnp.bfloat16)

    return middle(kernel, plan, pieces, [gate_w, up_w, down_w], [saved_gate, saved_up], (2,))


def per_device(act_fwd, grad_in, w_gate, w_up, w_down, saved_gate, saved_up, mask_fwd, mask_bwd):
    bundles = lax.axis_size("bundle")
    device = lax.axis_index("bundle")
    blocks_dev = act_fwd.shape[1] // BLOCK
    gate_w, up_w, down_w = w_gate[0], w_up[0], w_down[0]

    order = list(range(bundles - 1, -1, -1))
    half = bundles // 2
    near, far = range(1, half), range(bundles - 1, half - 1, -1)

    [packed_f] = pack(act_fwd[0], mask_fwd[0], device, blocks_dev)
    rows_f = swap(packed_f)
    packed_b = pack(after(grad_in[0], packed_f), mask_bwd[0], device, blocks_dev, order)
    packed_b = dict(zip(order, packed_b))
    base_b = shifted(after(grad_in[0], packed_b[0]), -1)
    next_mask_b = shifted(after(mask_bwd[0], packed_b[0]), -1)
    plan_f, plan_b, next_plan_b = plans_of(
        [mask_fwd[0], mask_bwd[0], next_mask_b], device, blocks_dev
    )

    rows_b = {0: packed_b[0]} | {o: permute(after(packed_b[o], base_b), o) for o in near}
    waits = [rows_b[o] for o in near]
    rows_b |= {o: permute(after(packed_b[o], *waits), o) for o in far}
    rows_b = [rows_b[o] for o in order]
    rows_f = after(rows_f, rows_b[0], next_plan_b)
    parts_f = forward(plan_f, rows_f, gate_w, up_w, down_w)
    back_f = swap(after(parts_f, *rows_b))
    parts_b = backward(
        plan_b, rows_b, gate_w, up_w, down_w, saved_gate[0], saved_up[0], order
    )
    parts_b = shifted(parts_b, -1)
    next_forward = copied(shifted(placed(plan_f, act_fwd[0], back_f, bundles), 1))
    back_b = swap(after(parts_b, back_f))
    next_backward = placed(next_plan_b, base_b, after(back_b, next_forward), bundles)
    return (next_forward[None], next_backward[None])


def solution(mesh):
    in_specs = (
        P("pipe", "bundle", None),
        P("pipe", "bundle", None),
        P("pipe", None, "bundle"),
        P("pipe", None, "bundle"),
        P("pipe", "bundle", None),
        P("pipe", None, "bundle"),
        P("pipe", None, "bundle"),
        P("pipe", None, None),
        P("pipe", None, None),
    )
    out_specs = (P("pipe", "bundle", None), P("pipe", "bundle", None))
    return jax.shard_map(
        per_device, mesh=mesh, in_specs=in_specs, out_specs=out_specs, check_vma=False
    )
```

```python
import jax
import jax.numpy as jnp
from jax import lax
from jax.experimental import pallas as pl
from jax.experimental.pallas import tpu as pltpu
from jax.sharding import PartitionSpec as P

BLOCK = 16
OUT, HAS, SAVED = range(3)
FIELDS = 3
VMEM_LIMIT = 48 * 1024 * 1024
VMEM_MOST = 60 * 1024 * 1024
VMEM_LEAST = 16 * 1024 * 1024
PLACE_CHUNK = 4096
ACROSS = ((1,), (1,))


def after(value, *others):
    return lax.optimization_barrier((value, others))[0]


def shifted(value, steps):
    count = lax.axis_size("pipe")
    return lax.ppermute(value, "pipe", [(p, (p + steps) % count) for p in range(count)])


def permute(piece, offset):
    count = lax.axis_size("bundle")
    return lax.ppermute(piece, "bundle", [(b, b ^ offset) for b in range(count)])


def swap(pieces):
    count = lax.axis_size("bundle")
    pieces = pieces.reshape(count, -1, pieces.shape[1])
    pieces = lax.all_to_all(pieces, "bundle", split_axis=0, concat_axis=0, tiled=True)
    return pieces.reshape(-1, pieces.shape[2])


def plan_one(bundles, blocks_dev, dev, mask, plan):
    def scan(source, bundle):
        active = at = jnp.int32(0)
        for j in range(blocks_dev):
            one = mask[bundle, source * blocks_dev + j]
            active, at = active + one, at + j * one
        return active, at

    for b in range(bundles):
        plan[HAS * bundles + b], plan[OUT * bundles + b] = scan(dev, b)
        plan[SAVED * bundles + b] = b * blocks_dev + scan(b, dev)[1]
    plan[FIELDS * bundles] = dev


def plans_of(masks, device, blocks_dev):
    bundles, number = masks[0].shape[1], len(masks)

    def kernel(dev_ref, *refs):
        for mask, plan in zip(refs[:number], refs[number:]):
            plan_one(bundles, blocks_dev, dev_ref[0], mask, plan)

    smem = pl.BlockSpec(memory_space=pltpu.SMEM)
    return pl.pallas_call(
        kernel,
        out_shape=[jax.ShapeDtypeStruct((FIELDS * bundles + 1,), jnp.int32)] * number,
        in_specs=[smem] * (1 + number),
        out_specs=[smem] * number,
    )(device[None], *[mask.T for mask in masks])


def chunk_of(width, most):
    chunk = min(width, most)
    while width % chunk:
        chunk //= 2
    return chunk


def chunked(kernel, plan, ins, out_rows, most, scratch=()):
    width = ins[0].shape[1]
    chunk = chunk_of(width, most)

    def spec(rows):
        return pl.BlockSpec((rows, chunk), lambda c, *_: (0, c))

    return pl.pallas_call(
        kernel,
        out_shape=jax.ShapeDtypeStruct((out_rows, width), jnp.bfloat16),
        grid_spec=pltpu.PrefetchScalarGridSpec(
            num_scalar_prefetch=1,
            grid=(width // chunk,),
            in_specs=[spec(a.shape[0]) for a in ins],
            out_specs=spec(out_rows),
            scratch_shapes=[pltpu.VMEM((r, chunk), t) for r, t in scratch],
        ),
        compiler_params=pltpu.CompilerParams(vmem_limit_bytes=VMEM_LEAST),
    )(plan, *ins)


def block_at(index):
    return pl.ds(pl.multiple_of(index * BLOCK, BLOCK), BLOCK)


def pack(rows, mask, device, blocks_dev, order=()):
    bundles, width = mask.shape[1], rows.shape[1]
    chunk = chunk_of(width, 4096)
    out_rows = [BLOCK] * bundles if order else [bundles * BLOCK]

    def kernel(dev_ref, mask_ref, rows_ref, *outs):
        for i in range(bundles):
            bundle = dev_ref[0] ^ order[i] if order else i
            at = jnp.int32(0)
            for j in range(1, blocks_dev):
                at += j * mask_ref[bundle, dev_ref[0] * blocks_dev + j]
            out = outs[i] if order else outs[0].at[pl.ds(i * BLOCK, BLOCK)]
            out[...] = rows_ref[block_at(at), :]

    return pl.pallas_call(
        kernel,
        out_shape=[jax.ShapeDtypeStruct((r, width), jnp.bfloat16) for r in out_rows],
        grid=(width // chunk,),
        in_specs=[
            pl.BlockSpec(memory_space=pltpu.SMEM),
            pl.BlockSpec(memory_space=pltpu.SMEM),
            pl.BlockSpec((rows.shape[0], chunk), lambda c: (0, c)),
        ],
        out_specs=[pl.BlockSpec((r, chunk), lambda c: (0, c)) for r in out_rows],
        compiler_params=pltpu.CompilerParams(vmem_limit_bytes=VMEM_MOST),
    )(device[None], mask.T, rows)


def placed(plan, base, parts, bundles):
    rows = base.shape[0]

    def kernel(plan_ref, base_ref, parts_ref, out):
        row = lax.broadcasted_iota(jnp.int32, (rows, bundles * BLOCK), 0)
        part = lax.broadcasted_iota(jnp.int32, (rows, bundles * BLOCK), 1)
        goes = jnp.full_like(row, -1)
        for b in range(bundles):
            first = plan_ref[OUT * bundles + b] * BLOCK - b * BLOCK
            held = (part >= b * BLOCK) & (part < (b + 1) * BLOCK) & (plan_ref[HAS * bundles + b] != 0)
            goes = jnp.where(held, part + first, goes)
        pick = jnp.where(goes == row, 1.0, 0.0).astype(jnp.bfloat16)
        total = base_ref[...].astype(jnp.float32) + dot(pick, parts_ref[...])
        out[...] = total.astype(jnp.bfloat16)

    return chunked(kernel, plan, [base, parts], rows, PLACE_CHUNK)


def copied(value):
    def kernel(value_ref, out):
        out[...] = value_ref[...]

    chunk = chunk_of(value.shape[1], 4096)
    spec = pl.BlockSpec((value.shape[0], chunk), lambda c: (0, c))
    return pl.pallas_call(
        kernel,
        out_shape=jax.ShapeDtypeStruct(value.shape, value.dtype),
        grid=(value.shape[1] // chunk,),
        in_specs=[spec],
        out_specs=spec,
        compiler_params=pltpu.CompilerParams(vmem_limit_bytes=VMEM_MOST),
    )(value)


def middle(kernel, plan, rows, weights, saved, first_weights):
    width = rows[0].shape[1]
    height = sum(piece.shape[0] for piece in rows)
    chunk = chunk_of(width, 4096)
    steps = width // chunk
    units = min(weights[0].shape)
    specs = [
        pl.BlockSpec((piece.shape[0], chunk), lambda s, c, *_: (0, jnp.where(s == 0, c, steps - 1)))
        for piece in rows
    ]
    for i, weight in enumerate(weights):
        tall = weight.shape[0] == width

        def at(s, c, *_, early=i in first_weights, tall=tall):
            where = jnp.where(s == 0, c, steps - 1) if early else jnp.where(s == 0, 0, c)
            return (where, 0) if tall else (0, where)

        shape = (chunk, weight.shape[1]) if tall else (weight.shape[0], chunk)
        specs.append(pl.BlockSpec(shape, at))
    specs += [pl.BlockSpec(a.shape, lambda s, c, *_: (0, 0)) for a in saved]
    return pl.pallas_call(
        kernel,
        out_shape=jax.ShapeDtypeStruct((height, width), jnp.bfloat16),
        grid_spec=pltpu.PrefetchScalarGridSpec(
            num_scalar_prefetch=1,
            grid=(2, steps),
            in_specs=specs,
            out_specs=pl.BlockSpec((height, chunk), lambda s, c, *_: (0, jnp.where(s == 0, 0, c))),
            scratch_shapes=[
                pltpu.VMEM((height, chunk), jnp.bfloat16),
                pltpu.VMEM((height, 2 * units), jnp.float32),
                pltpu.VMEM((height, 2 * units), jnp.bfloat16),
            ],
        ),
        compiler_params=pltpu.CompilerParams(vmem_limit_bytes=VMEM_LIMIT),
    )(plan, *rows, *weights, *saved)


def dot(left, right, dims=((1,), (0,))):
    return lax.dot_general(left, right, (dims, ((), ())), preferred_element_type=jnp.float32)


def forward(plan, rows, gate_w, up_w, down_w):
    units = gate_w.shape[1]

    def kernel(plan_ref, rows_ref, gate_ref, up_ref, down_ref, out, _, total_ref, hidden_ref):
        first, start = pl.program_id(0) == 0, pl.program_id(1) == 0

        @pl.when(first & start)
        def _():
            total_ref[...] = jnp.zeros_like(total_ref)

        @pl.when(first)
        def _():
            total_ref[:, :units] += dot(rows_ref[...], gate_ref[...])
            total_ref[:, units:] += dot(rows_ref[...], up_ref[...])

        @pl.when(jnp.logical_not(first) & start)
        def _():
            hidden = jnp.maximum(total_ref[:, :units], 0.0) * total_ref[:, units:]
            hidden_ref[:, :units] = hidden.astype(jnp.bfloat16)

        @pl.when(jnp.logical_not(first))
        def _():
            out[...] = dot(hidden_ref[:, :units], down_ref[...]).astype(jnp.bfloat16)

    return middle(kernel, plan, [rows], [gate_w, up_w, down_w], [], (0, 1))


def backward(plan, pieces, gate_w, up_w, down_w, saved_gate, saved_up, order):
    bundles = len(order)
    units = gate_w.shape[1]

    def kernel(plan_ref, *refs):
        ins, refs = refs[:bundles], refs[bundles:]
        gate_ref, up_ref, down_ref, gate_saved, up_saved, out, rows_ref, total_ref, grad_ref = refs
        first, start = pl.program_id(0) == 0, pl.program_id(1) == 0

        @pl.when(first & start)
        def _():
            total_ref[...] = jnp.zeros_like(total_ref)

        @pl.when(first)
        def _():
            for i, piece in enumerate(ins):
                at = block_at(plan_ref[FIELDS * bundles] ^ order[i])
                rows_ref[at, :] = piece[...]
            total_ref[:, :units] += dot(rows_ref[...], down_ref[...], ACROSS)

        @pl.when(jnp.logical_not(first) & start)
        def _():
            for b in range(bundles):
                place, at = pl.ds(b * BLOCK, BLOCK), block_at(plan_ref[SAVED * bundles + b])
                gate = gate_saved[at, :].astype(jnp.float32)
                up = up_saved[at, :].astype(jnp.float32)
                grad = total_ref[place, :units]
                grad_gate = jnp.where(gate > 0, grad * up, 0.0)
                grad_ref[place, :units] = grad_gate.astype(jnp.bfloat16)
                grad_ref[place, units:] = (grad * jnp.maximum(gate, 0.0)).astype(jnp.bfloat16)

        @pl.when(jnp.logical_not(first))
        def _():
            total = dot(grad_ref[:, :units], gate_ref[...], ACROSS)
            total += dot(grad_ref[:, units:], up_ref[...], ACROSS)
            out[...] = total.astype(jnp.bfloat16)

    return middle(kernel, plan, pieces, [gate_w, up_w, down_w], [saved_gate, saved_up], (2,))


def per_device(act_fwd, grad_in, w_gate, w_up, w_down, saved_gate, saved_up, mask_fwd, mask_bwd):
    bundles = lax.axis_size("bundle")
    device = lax.axis_index("bundle")
    blocks_dev = act_fwd.shape[1] // BLOCK
    gate_w, up_w, down_w = w_gate[0], w_up[0], w_down[0]

    order = list(range(bundles - 1, -1, -1))
    half = bundles // 2
    near, far = range(1, half), range(bundles - 1, half - 1, -1)

    [packed_f] = pack(act_fwd[0], mask_fwd[0], device, blocks_dev)
    rows_f = swap(packed_f)
    packed_b = pack(after(grad_in[0], packed_f), mask_bwd[0], device, blocks_dev, order)
    packed_b = dict(zip(order, packed_b))
    base_b = shifted(after(grad_in[0], packed_b[0]), -1)
    next_mask_b = shifted(after(mask_bwd[0], packed_b[0]), -1)
    plan_f, plan_b, next_plan_b = plans_of(
        [mask_fwd[0], mask_bwd[0], next_mask_b], device, blocks_dev
    )

    rows_b = {0: packed_b[0]} | {o: permute(after(packed_b[o], base_b), o) for o in near}
    waits = [rows_b[1]]
    rows_b |= {o: permute(after(packed_b[o], *waits), o) for o in far}
    rows_b = [rows_b[o] for o in order]
    rows_f = after(rows_f, rows_b[0], next_plan_b)
    parts_f = forward(plan_f, rows_f, gate_w, up_w, down_w)
    back_f = swap(after(parts_f, *rows_b))
    parts_b = backward(
        plan_b, rows_b, gate_w, up_w, down_w, saved_gate[0], saved_up[0], order
    )
    parts_b = shifted(parts_b, -1)
    next_forward = copied(shifted(placed(plan_f, act_fwd[0], back_f, bundles), 1))
    back_b = swap(after(parts_b, back_f))
    next_backward = placed(next_plan_b, base_b, after(back_b, next_forward), bundles)
    return (next_forward[None], next_backward[None])


def solution(mesh):
    in_specs = (
        P("pipe", "bundle", None),
        P("pipe", "bundle", None),
        P("pipe", None, "bundle"),
        P("pipe", None, "bundle"),
        P("pipe", "bundle", None),
        P("pipe", None, "bundle"),
        P("pipe", None, "bundle"),
        P("pipe", None, None),
        P("pipe", None, None),
    )
    out_specs = (P("pipe", "bundle", None), P("pipe", "bundle", None))
    return jax.shard_map(
        per_device, mesh=mesh, in_specs=in_specs, out_specs=out_specs, check_vma=False
    )
```

```python
import jax
import jax.numpy as jnp
from jax import lax
from jax.experimental import pallas as pl
from jax.experimental.pallas import tpu as pltpu
from jax.sharding import PartitionSpec as P

BLOCK = 16
OUT, HAS, SAVED = range(3)
FIELDS = 3
VMEM_LIMIT = 60 * 1024 * 1024
VMEM_MOST = 60 * 1024 * 1024
VMEM_LEAST = 16 * 1024 * 1024
PLACE_CHUNK = 4096
ACROSS = ((1,), (1,))


def after(value, *others):
    return lax.optimization_barrier((value, others))[0]


def shifted(value, steps):
    count = lax.axis_size("pipe")
    return lax.ppermute(value, "pipe", [(p, (p + steps) % count) for p in range(count)])


def permute(piece, offset):
    count = lax.axis_size("bundle")
    return lax.ppermute(piece, "bundle", [(b, b ^ offset) for b in range(count)])


def swap(pieces):
    count = lax.axis_size("bundle")
    pieces = pieces.reshape(count, -1, pieces.shape[1])
    pieces = lax.all_to_all(pieces, "bundle", split_axis=0, concat_axis=0, tiled=True)
    return pieces.reshape(-1, pieces.shape[2])


def plan_one(bundles, blocks_dev, dev, mask, plan):
    def scan(source, bundle):
        active = at = jnp.int32(0)
        for j in range(blocks_dev):
            one = mask[bundle, source * blocks_dev + j]
            active, at = active + one, at + j * one
        return active, at

    for b in range(bundles):
        plan[HAS * bundles + b], plan[OUT * bundles + b] = scan(dev, b)
        plan[SAVED * bundles + b] = b * blocks_dev + scan(b, dev)[1]
    plan[FIELDS * bundles] = dev


def plans_of(masks, device, blocks_dev):
    bundles, number = masks[0].shape[1], len(masks)

    def kernel(dev_ref, *refs):
        for mask, plan in zip(refs[:number], refs[number:]):
            plan_one(bundles, blocks_dev, dev_ref[0], mask, plan)

    smem = pl.BlockSpec(memory_space=pltpu.SMEM)
    return pl.pallas_call(
        kernel,
        out_shape=[jax.ShapeDtypeStruct((FIELDS * bundles + 1,), jnp.int32)] * number,
        in_specs=[smem] * (1 + number),
        out_specs=[smem] * number,
    )(device[None], *[mask.T for mask in masks])


def chunk_of(width, most):
    chunk = min(width, most)
    while width % chunk:
        chunk //= 2
    return chunk


def chunked(kernel, plan, ins, out_rows, most, scratch=()):
    width = ins[0].shape[1]
    chunk = chunk_of(width, most)

    def spec(rows):
        return pl.BlockSpec((rows, chunk), lambda c, *_: (0, c))

    return pl.pallas_call(
        kernel,
        out_shape=jax.ShapeDtypeStruct((out_rows, width), jnp.bfloat16),
        grid_spec=pltpu.PrefetchScalarGridSpec(
            num_scalar_prefetch=1,
            grid=(width // chunk,),
            in_specs=[spec(a.shape[0]) for a in ins],
            out_specs=spec(out_rows),
            scratch_shapes=[pltpu.VMEM((r, chunk), t) for r, t in scratch],
        ),
        compiler_params=pltpu.CompilerParams(vmem_limit_bytes=VMEM_LEAST),
    )(plan, *ins)


def block_at(index):
    return pl.ds(pl.multiple_of(index * BLOCK, BLOCK), BLOCK)


def pack(rows, mask, device, blocks_dev, order=()):
    bundles, width = mask.shape[1], rows.shape[1]
    chunk = chunk_of(width, 4096)
    out_rows = [BLOCK] * bundles if order else [bundles * BLOCK]

    def kernel(dev_ref, mask_ref, rows_ref, *outs):
        for i in range(bundles):
            bundle = dev_ref[0] ^ order[i] if order else i
            at = jnp.int32(0)
            for j in range(1, blocks_dev):
                at += j * mask_ref[bundle, dev_ref[0] * blocks_dev + j]
            out = outs[i] if order else outs[0].at[pl.ds(i * BLOCK, BLOCK)]
            out[...] = rows_ref[block_at(at), :]

    return pl.pallas_call(
        kernel,
        out_shape=[jax.ShapeDtypeStruct((r, width), jnp.bfloat16) for r in out_rows],
        grid=(width // chunk,),
        in_specs=[
            pl.BlockSpec(memory_space=pltpu.SMEM),
            pl.BlockSpec(memory_space=pltpu.SMEM),
            pl.BlockSpec((rows.shape[0], chunk), lambda c: (0, c)),
        ],
        out_specs=[pl.BlockSpec((r, chunk), lambda c: (0, c)) for r in out_rows],
        compiler_params=pltpu.CompilerParams(vmem_limit_bytes=VMEM_MOST),
    )(device[None], mask.T, rows)


def placed(plan, base, parts, bundles):
    rows = base.shape[0]

    def kernel(plan_ref, base_ref, parts_ref, out):
        row = lax.broadcasted_iota(jnp.int32, (rows, bundles * BLOCK), 0)
        part = lax.broadcasted_iota(jnp.int32, (rows, bundles * BLOCK), 1)
        goes = jnp.full_like(row, -1)
        for b in range(bundles):
            first = plan_ref[OUT * bundles + b] * BLOCK - b * BLOCK
            held = (part >= b * BLOCK) & (part < (b + 1) * BLOCK) & (plan_ref[HAS * bundles + b] != 0)
            goes = jnp.where(held, part + first, goes)
        pick = jnp.where(goes == row, 1.0, 0.0).astype(jnp.bfloat16)
        total = base_ref[...].astype(jnp.float32) + dot(pick, parts_ref[...])
        out[...] = total.astype(jnp.bfloat16)

    return chunked(kernel, plan, [base, parts], rows, PLACE_CHUNK)


def copied(value):
    def kernel(value_ref, out):
        out[...] = value_ref[...]

    chunk = chunk_of(value.shape[1], 4096)
    spec = pl.BlockSpec((value.shape[0], chunk), lambda c: (0, c))
    return pl.pallas_call(
        kernel,
        out_shape=jax.ShapeDtypeStruct(value.shape, value.dtype),
        grid=(value.shape[1] // chunk,),
        in_specs=[spec],
        out_specs=spec,
        compiler_params=pltpu.CompilerParams(vmem_limit_bytes=VMEM_MOST),
    )(value)


def middle(kernel, plan, rows, weights, saved, first_weights):
    width = rows[0].shape[1]
    height = sum(piece.shape[0] for piece in rows)
    chunk = chunk_of(width, 4096)
    steps = width // chunk
    units = min(weights[0].shape)
    specs = [
        pl.BlockSpec((piece.shape[0], chunk), lambda s, c, *_: (0, jnp.where(s == 0, c, steps - 1)))
        for piece in rows
    ]
    for i, weight in enumerate(weights):
        tall = weight.shape[0] == width

        def at(s, c, *_, early=i in first_weights, tall=tall):
            where = jnp.where(s == 0, c, steps - 1) if early else jnp.where(s == 0, 0, c)
            return (where, 0) if tall else (0, where)

        shape = (chunk, weight.shape[1]) if tall else (weight.shape[0], chunk)
        specs.append(pl.BlockSpec(shape, at))
    specs += [pl.BlockSpec(a.shape, lambda s, c, *_: (0, 0)) for a in saved]
    return pl.pallas_call(
        kernel,
        out_shape=jax.ShapeDtypeStruct((height, width), jnp.bfloat16),
        grid_spec=pltpu.PrefetchScalarGridSpec(
            num_scalar_prefetch=1,
            grid=(2, steps),
            in_specs=specs,
            out_specs=pl.BlockSpec((height, chunk), lambda s, c, *_: (0, jnp.where(s == 0, 0, c))),
            scratch_shapes=[
                pltpu.VMEM((height, chunk), jnp.bfloat16),
                pltpu.VMEM((height, 2 * units), jnp.float32),
                pltpu.VMEM((height, 2 * units), jnp.bfloat16),
            ],
        ),
        compiler_params=pltpu.CompilerParams(vmem_limit_bytes=VMEM_LIMIT),
    )(plan, *rows, *weights, *saved)


def dot(left, right, dims=((1,), (0,))):
    return lax.dot_general(left, right, (dims, ((), ())), preferred_element_type=jnp.float32)


def forward(plan, rows, gate_w, up_w, down_w):
    units = gate_w.shape[1]

    def kernel(plan_ref, rows_ref, gate_ref, up_ref, down_ref, out, _, total_ref, hidden_ref):
        first, start = pl.program_id(0) == 0, pl.program_id(1) == 0

        @pl.when(first & start)
        def _():
            total_ref[...] = jnp.zeros_like(total_ref)

        @pl.when(first)
        def _():
            total_ref[:, :units] += dot(rows_ref[...], gate_ref[...])
            total_ref[:, units:] += dot(rows_ref[...], up_ref[...])

        @pl.when(jnp.logical_not(first) & start)
        def _():
            hidden = jnp.maximum(total_ref[:, :units], 0.0) * total_ref[:, units:]
            hidden_ref[:, :units] = hidden.astype(jnp.bfloat16)

        @pl.when(jnp.logical_not(first))
        def _():
            out[...] = dot(hidden_ref[:, :units], down_ref[...]).astype(jnp.bfloat16)

    return middle(kernel, plan, [rows], [gate_w, up_w, down_w], [], (0, 1))


def backward(plan, pieces, gate_w, up_w, down_w, saved_gate, saved_up, order):
    bundles = len(order)
    units = gate_w.shape[1]

    def kernel(plan_ref, *refs):
        ins, refs = refs[:bundles], refs[bundles:]
        gate_ref, up_ref, down_ref, gate_saved, up_saved, out, rows_ref, total_ref, grad_ref = refs
        first, start = pl.program_id(0) == 0, pl.program_id(1) == 0

        @pl.when(first & start)
        def _():
            total_ref[...] = jnp.zeros_like(total_ref)

        @pl.when(first)
        def _():
            for i, piece in enumerate(ins):
                at = block_at(plan_ref[FIELDS * bundles] ^ order[i])
                rows_ref[at, :] = piece[...]
            total_ref[:, :units] += dot(rows_ref[...], down_ref[...], ACROSS)

        @pl.when(jnp.logical_not(first) & start)
        def _():
            for b in range(bundles):
                place, at = pl.ds(b * BLOCK, BLOCK), block_at(plan_ref[SAVED * bundles + b])
                gate = gate_saved[at, :].astype(jnp.float32)
                up = up_saved[at, :].astype(jnp.float32)
                grad = total_ref[place, :units]
                grad_gate = jnp.where(gate > 0, grad * up, 0.0)
                grad_ref[place, :units] = grad_gate.astype(jnp.bfloat16)
                grad_ref[place, units:] = (grad * jnp.maximum(gate, 0.0)).astype(jnp.bfloat16)

        @pl.when(jnp.logical_not(first))
        def _():
            total = dot(grad_ref[:, :units], gate_ref[...], ACROSS)
            total += dot(grad_ref[:, units:], up_ref[...], ACROSS)
            out[...] = total.astype(jnp.bfloat16)

    return middle(kernel, plan, pieces, [gate_w, up_w, down_w], [saved_gate, saved_up], (2,))


def per_device(act_fwd, grad_in, w_gate, w_up, w_down, saved_gate, saved_up, mask_fwd, mask_bwd):
    bundles = lax.axis_size("bundle")
    device = lax.axis_index("bundle")
    blocks_dev = act_fwd.shape[1] // BLOCK
    gate_w, up_w, down_w = w_gate[0], w_up[0], w_down[0]

    order = list(range(bundles - 1, -1, -1))
    half = bundles // 2
    near, far = range(1, half), range(bundles - 1, half - 1, -1)

    [packed_f] = pack(act_fwd[0], mask_fwd[0], device, blocks_dev)
    rows_f = swap(packed_f)
    packed_b = pack(after(grad_in[0], packed_f), mask_bwd[0], device, blocks_dev, order)
    packed_b = dict(zip(order, packed_b))
    base_b = shifted(after(grad_in[0], packed_b[0]), -1)
    next_mask_b = shifted(after(mask_bwd[0], packed_b[0]), -1)
    plan_f, plan_b, next_plan_b = plans_of(
        [mask_fwd[0], mask_bwd[0], next_mask_b], device, blocks_dev
    )

    rows_b = {0: packed_b[0]} | {o: permute(after(packed_b[o], base_b), o) for o in near}
    waits = [rows_b[1]]
    rows_b |= {o: permute(after(packed_b[o], *waits), o) for o in far}
    rows_b = [rows_b[o] for o in order]
    rows_f = after(rows_f, rows_b[0], next_plan_b)
    parts_f = forward(plan_f, rows_f, gate_w, up_w, down_w)
    back_f = swap(after(parts_f, *rows_b))
    parts_b = backward(
        plan_b, rows_b, gate_w, up_w, down_w, saved_gate[0], saved_up[0], order
    )
    parts_b = shifted(parts_b, -1)
    next_forward = copied(shifted(placed(plan_f, act_fwd[0], back_f, bundles), 1))
    back_b = swap(after(parts_b, back_f))
    next_backward = placed(next_plan_b, base_b, after(back_b, next_forward), bundles)
    return (next_forward[None], next_backward[None])


def solution(mesh):
    in_specs = (
        P("pipe", "bundle", None),
        P("pipe", "bundle", None),
        P("pipe", None, "bundle"),
        P("pipe", None, "bundle"),
        P("pipe", "bundle", None),
        P("pipe", None, "bundle"),
        P("pipe", None, "bundle"),
        P("pipe", None, None),
        P("pipe", None, None),
    )
    out_specs = (P("pipe", "bundle", None), P("pipe", "bundle", None))
    return jax.shard_map(
        per_device, mesh=mesh, in_specs=in_specs, out_specs=out_specs, check_vma=False
    )
```

```python
import jax
import jax.numpy as jnp
from jax import lax
from jax.experimental import pallas as pl
from jax.experimental.pallas import tpu as pltpu
from jax.sharding import PartitionSpec as P

BLOCK = 16
OUT, HAS, SAVED = range(3)
FIELDS = 3
VMEM_LIMIT = 60 * 1024 * 1024
VMEM_MOST = 60 * 1024 * 1024
VMEM_LEAST = 10 * 1024 * 1024
PLACE_CHUNK = 4096
ACROSS = ((1,), (1,))


def after(value, *others):
    return lax.optimization_barrier((value, others))[0]


def shifted(value, steps):
    count = lax.axis_size("pipe")
    return lax.ppermute(value, "pipe", [(p, (p + steps) % count) for p in range(count)])


def permute(piece, offset):
    count = lax.axis_size("bundle")
    return lax.ppermute(piece, "bundle", [(b, b ^ offset) for b in range(count)])


def swap(pieces):
    count = lax.axis_size("bundle")
    pieces = pieces.reshape(count, -1, pieces.shape[1])
    pieces = lax.all_to_all(pieces, "bundle", split_axis=0, concat_axis=0, tiled=True)
    return pieces.reshape(-1, pieces.shape[2])


def plan_one(bundles, blocks_dev, dev, mask, plan):
    def scan(source, bundle):
        active = at = jnp.int32(0)
        for j in range(blocks_dev):
            one = mask[bundle, source * blocks_dev + j]
            active, at = active + one, at + j * one
        return active, at

    for b in range(bundles):
        plan[HAS * bundles + b], plan[OUT * bundles + b] = scan(dev, b)
        plan[SAVED * bundles + b] = b * blocks_dev + scan(b, dev)[1]
    plan[FIELDS * bundles] = dev


def plans_of(masks, device, blocks_dev):
    bundles, number = masks[0].shape[1], len(masks)

    def kernel(dev_ref, *refs):
        for mask, plan in zip(refs[:number], refs[number:]):
            plan_one(bundles, blocks_dev, dev_ref[0], mask, plan)

    smem = pl.BlockSpec(memory_space=pltpu.SMEM)
    return pl.pallas_call(
        kernel,
        out_shape=[jax.ShapeDtypeStruct((FIELDS * bundles + 1,), jnp.int32)] * number,
        in_specs=[smem] * (1 + number),
        out_specs=[smem] * number,
    )(device[None], *[mask.T for mask in masks])


def chunk_of(width, most):
    chunk = min(width, most)
    while width % chunk:
        chunk //= 2
    return chunk


def chunked(kernel, plan, ins, out_rows, most, scratch=()):
    width = ins[0].shape[1]
    chunk = chunk_of(width, most)

    def spec(rows):
        return pl.BlockSpec((rows, chunk), lambda c, *_: (0, c))

    return pl.pallas_call(
        kernel,
        out_shape=jax.ShapeDtypeStruct((out_rows, width), jnp.bfloat16),
        grid_spec=pltpu.PrefetchScalarGridSpec(
            num_scalar_prefetch=1,
            grid=(width // chunk,),
            in_specs=[spec(a.shape[0]) for a in ins],
            out_specs=spec(out_rows),
            scratch_shapes=[pltpu.VMEM((r, chunk), t) for r, t in scratch],
        ),
        compiler_params=pltpu.CompilerParams(vmem_limit_bytes=VMEM_LEAST),
    )(plan, *ins)


def block_at(index):
    return pl.ds(pl.multiple_of(index * BLOCK, BLOCK), BLOCK)


def pack(rows, mask, device, blocks_dev, order=()):
    bundles, width = mask.shape[1], rows.shape[1]
    chunk = chunk_of(width, 4096)
    out_rows = [BLOCK] * bundles if order else [bundles * BLOCK]

    def kernel(dev_ref, mask_ref, rows_ref, *outs):
        for i in range(bundles):
            bundle = dev_ref[0] ^ order[i] if order else i
            at = jnp.int32(0)
            for j in range(1, blocks_dev):
                at += j * mask_ref[bundle, dev_ref[0] * blocks_dev + j]
            out = outs[i] if order else outs[0].at[pl.ds(i * BLOCK, BLOCK)]
            out[...] = rows_ref[block_at(at), :]

    return pl.pallas_call(
        kernel,
        out_shape=[jax.ShapeDtypeStruct((r, width), jnp.bfloat16) for r in out_rows],
        grid=(width // chunk,),
        in_specs=[
            pl.BlockSpec(memory_space=pltpu.SMEM),
            pl.BlockSpec(memory_space=pltpu.SMEM),
            pl.BlockSpec((rows.shape[0], chunk), lambda c: (0, c)),
        ],
        out_specs=[pl.BlockSpec((r, chunk), lambda c: (0, c)) for r in out_rows],
        compiler_params=pltpu.CompilerParams(vmem_limit_bytes=VMEM_MOST),
    )(device[None], mask.T, rows)


def placed(plan, base, parts, bundles):
    rows = base.shape[0]

    def kernel(plan_ref, base_ref, parts_ref, out):
        row = lax.broadcasted_iota(jnp.int32, (rows, bundles * BLOCK), 0)
        part = lax.broadcasted_iota(jnp.int32, (rows, bundles * BLOCK), 1)
        goes = jnp.full_like(row, -1)
        for b in range(bundles):
            first = plan_ref[OUT * bundles + b] * BLOCK - b * BLOCK
            held = (part >= b * BLOCK) & (part < (b + 1) * BLOCK) & (plan_ref[HAS * bundles + b] != 0)
            goes = jnp.where(held, part + first, goes)
        pick = jnp.where(goes == row, 1.0, 0.0).astype(jnp.bfloat16)
        total = base_ref[...].astype(jnp.float32) + dot(pick, parts_ref[...])
        out[...] = total.astype(jnp.bfloat16)

    return chunked(kernel, plan, [base, parts], rows, PLACE_CHUNK)


def copied(value):
    def kernel(value_ref, out):
        out[...] = value_ref[...]

    chunk = chunk_of(value.shape[1], 4096)
    spec = pl.BlockSpec((value.shape[0], chunk), lambda c: (0, c))
    return pl.pallas_call(
        kernel,
        out_shape=jax.ShapeDtypeStruct(value.shape, value.dtype),
        grid=(value.shape[1] // chunk,),
        in_specs=[spec],
        out_specs=spec,
        compiler_params=pltpu.CompilerParams(vmem_limit_bytes=VMEM_MOST),
    )(value)


def middle(kernel, plan, rows, weights, saved, first_weights):
    width = rows[0].shape[1]
    height = sum(piece.shape[0] for piece in rows)
    chunk = chunk_of(width, 4096)
    steps = width // chunk
    units = min(weights[0].shape)
    specs = [
        pl.BlockSpec((piece.shape[0], chunk), lambda s, c, *_: (0, jnp.where(s == 0, c, steps - 1)))
        for piece in rows
    ]
    for i, weight in enumerate(weights):
        tall = weight.shape[0] == width

        def at(s, c, *_, early=i in first_weights, tall=tall):
            where = jnp.where(s == 0, c, steps - 1) if early else jnp.where(s == 0, 0, c)
            return (where, 0) if tall else (0, where)

        shape = (chunk, weight.shape[1]) if tall else (weight.shape[0], chunk)
        specs.append(pl.BlockSpec(shape, at))
    specs += [pl.BlockSpec(a.shape, lambda s, c, *_: (0, 0)) for a in saved]
    return pl.pallas_call(
        kernel,
        out_shape=jax.ShapeDtypeStruct((height, width), jnp.bfloat16),
        grid_spec=pltpu.PrefetchScalarGridSpec(
            num_scalar_prefetch=1,
            grid=(2, steps),
            in_specs=specs,
            out_specs=pl.BlockSpec((height, chunk), lambda s, c, *_: (0, jnp.where(s == 0, 0, c))),
            scratch_shapes=[
                pltpu.VMEM((height, chunk), jnp.bfloat16),
                pltpu.VMEM((height, 2 * units), jnp.float32),
                pltpu.VMEM((height, 2 * units), jnp.bfloat16),
            ],
        ),
        compiler_params=pltpu.CompilerParams(vmem_limit_bytes=VMEM_LIMIT),
    )(plan, *rows, *weights, *saved)


def dot(left, right, dims=((1,), (0,))):
    return lax.dot_general(left, right, (dims, ((), ())), preferred_element_type=jnp.float32)


def forward(plan, rows, gate_w, up_w, down_w):
    units = gate_w.shape[1]

    def kernel(plan_ref, rows_ref, gate_ref, up_ref, down_ref, out, _, total_ref, hidden_ref):
        first, start = pl.program_id(0) == 0, pl.program_id(1) == 0

        @pl.when(first & start)
        def _():
            total_ref[...] = jnp.zeros_like(total_ref)

        @pl.when(first)
        def _():
            total_ref[:, :units] += dot(rows_ref[...], gate_ref[...])
            total_ref[:, units:] += dot(rows_ref[...], up_ref[...])

        @pl.when(jnp.logical_not(first) & start)
        def _():
            hidden = jnp.maximum(total_ref[:, :units], 0.0) * total_ref[:, units:]
            hidden_ref[:, :units] = hidden.astype(jnp.bfloat16)

        @pl.when(jnp.logical_not(first))
        def _():
            out[...] = dot(hidden_ref[:, :units], down_ref[...]).astype(jnp.bfloat16)

    return middle(kernel, plan, [rows], [gate_w, up_w, down_w], [], (0, 1))


def backward(plan, pieces, gate_w, up_w, down_w, saved_gate, saved_up, order):
    bundles = len(order)
    units = gate_w.shape[1]

    def kernel(plan_ref, *refs):
        ins, refs = refs[:bundles], refs[bundles:]
        gate_ref, up_ref, down_ref, gate_saved, up_saved, out, rows_ref, total_ref, grad_ref = refs
        first, start = pl.program_id(0) == 0, pl.program_id(1) == 0

        @pl.when(first & start)
        def _():
            total_ref[...] = jnp.zeros_like(total_ref)

        @pl.when(first)
        def _():
            for i, piece in enumerate(ins):
                at = block_at(plan_ref[FIELDS * bundles] ^ order[i])
                rows_ref[at, :] = piece[...]
            total_ref[:, :units] += dot(rows_ref[...], down_ref[...], ACROSS)

        @pl.when(jnp.logical_not(first) & start)
        def _():
            for b in range(bundles):
                place, at = pl.ds(b * BLOCK, BLOCK), block_at(plan_ref[SAVED * bundles + b])
                gate = gate_saved[at, :].astype(jnp.float32)
                up = up_saved[at, :].astype(jnp.float32)
                grad = total_ref[place, :units]
                grad_gate = jnp.where(gate > 0, grad * up, 0.0)
                grad_ref[place, :units] = grad_gate.astype(jnp.bfloat16)
                grad_ref[place, units:] = (grad * jnp.maximum(gate, 0.0)).astype(jnp.bfloat16)

        @pl.when(jnp.logical_not(first))
        def _():
            total = dot(grad_ref[:, :units], gate_ref[...], ACROSS)
            total += dot(grad_ref[:, units:], up_ref[...], ACROSS)
            out[...] = total.astype(jnp.bfloat16)

    return middle(kernel, plan, pieces, [gate_w, up_w, down_w], [saved_gate, saved_up], (2,))


def per_device(act_fwd, grad_in, w_gate, w_up, w_down, saved_gate, saved_up, mask_fwd, mask_bwd):
    bundles = lax.axis_size("bundle")
    device = lax.axis_index("bundle")
    blocks_dev = act_fwd.shape[1] // BLOCK
    gate_w, up_w, down_w = w_gate[0], w_up[0], w_down[0]

    order = list(range(bundles - 1, -1, -1))
    half = bundles // 2
    near, far = range(1, half), range(bundles - 1, half - 1, -1)

    [packed_f] = pack(act_fwd[0], mask_fwd[0], device, blocks_dev)
    rows_f = swap(packed_f)
    packed_b = pack(after(grad_in[0], packed_f), mask_bwd[0], device, blocks_dev, order)
    packed_b = dict(zip(order, packed_b))
    base_b = shifted(after(grad_in[0], packed_b[0]), -1)
    next_mask_b = shifted(after(mask_bwd[0], packed_b[0]), -1)
    plan_f, plan_b, next_plan_b = plans_of(
        [mask_fwd[0], mask_bwd[0], next_mask_b], device, blocks_dev
    )

    rows_b = {0: packed_b[0]} | {o: permute(after(packed_b[o], base_b), o) for o in near}
    waits = [rows_b[1]]
    rows_b |= {o: permute(after(packed_b[o], *waits), o) for o in far}
    rows_b = [rows_b[o] for o in order]
    rows_f = after(rows_f, rows_b[0], next_plan_b)
    parts_f = forward(plan_f, rows_f, gate_w, up_w, down_w)
    back_f = swap(after(parts_f, *rows_b))
    parts_b = backward(
        plan_b, rows_b, gate_w, up_w, down_w, saved_gate[0], saved_up[0], order
    )
    parts_b = shifted(parts_b, -1)
    next_forward = copied(shifted(placed(plan_f, act_fwd[0], back_f, bundles), 1))
    back_b = swap(after(parts_b, back_f))
    next_backward = placed(next_plan_b, base_b, after(back_b, next_forward), bundles)
    return (next_forward[None], next_backward[None])


def solution(mesh):
    in_specs = (
        P("pipe", "bundle", None),
        P("pipe", "bundle", None),
        P("pipe", None, "bundle"),
        P("pipe", None, "bundle"),
        P("pipe", "bundle", None),
        P("pipe", None, "bundle"),
        P("pipe", None, "bundle"),
        P("pipe", None, None),
        P("pipe", None, None),
    )
    out_specs = (P("pipe", "bundle", None), P("pipe", "bundle", None))
    return jax.shard_map(
        per_device, mesh=mesh, in_specs=in_specs, out_specs=out_specs, check_vma=False
    )
```
